32 devices in a mesh: gx: 8 (over z, y), yz: 4 (over x, core).
Axes of the slice: x: 2, y: 2, z: 4, core: 2. Of those that a mesh axis runs over, the one named last changes fastest.
Arguments:
- field: float32 [512, 512, 1024], P('gx', None, 'yz'), may hold values from -58 to 58, as said below
- start: float32 [512, 128], replicated, may hold values from -6 to 6
Outputs:
- basis: float32 [512, 128], replicated
- gram_y: float32 [1024, 1024], P('yz', 'gx')
The draws below stay inside these ranges and needn't reach their ends.
Inputs may be any that keep to these rules, and one draw needn't show every extreme that they name: `field`: every cell is a real number at most a few tens in magnitude.
All inputs are finite; a program needn't handle non-finite values.
Results may differ from the reference program's by a relative error of at most 0.00025.
Values sent between devices are 32-bit elements; how exact they have to be, the bound alone decides.
No kernel may reach another device: no remote copies, remote signals or barrier semaphores. Data moves between devices by JAX's collectives and lax.ppermute only.
A program may use at most 192 MiB of HBM per device.

```python
import math
import jax
import jax.numpy as jnp
from jax import lax

NX = 512
NY = 1024
RANK = 128
NZ = 512
ITERS = 4


def draw_field(key, part):
    key = jax.random.fold_in(key, 11)
    first, second, third = jax.random.split(key, 3)
    noise = jnp.clip(jax.random.normal(first, (NX, NZ, NY), jnp.float32), -6.0, 6.0)
    row_scale = jnp.exp(jax.random.uniform(second, (NX, 1, 1), jnp.float32, 0.0, math.log(3.0)))
    fibre_scale = jnp.exp(jax.random.uniform(third, (1, NZ, NY), jnp.float32, 0.0, math.log(2.0)))
    mixed = noise + 0.6 * jnp.roll(noise, 1, axis=0)
    return row_scale * fibre_scale * mixed


def centred(key, shape, spread, limit, dtype=jnp.bfloat16):
    values = jax.random.normal(key, shape, jnp.float32) * spread
    return jnp.minimum(jnp.maximum(values, -limit), limit).astype(dtype)


def setup_inputs(seed: int = 0) -> dict:
    streams_of = jax.random.split(jax.random.key(seed), 3)
    return {
        "field": draw_field(jax.random.fold_in(streams_of[2], 71), 0),
        "start": centred(streams_of[1], (NX, RANK), 1.0, 6.0, jnp.float32),
    }


def orthonormal(product):
    cross = jnp.dot(product.T.astype(jnp.float32), product.astype(jnp.float32), precision=lax.Precision.HIGHEST, preferred_element_type=jnp.float32)
    lower = lax.linalg.cholesky(cross)
    return lax.linalg.triangular_solve(lower, product, left_side=False, lower=True, transpose_a=True)

def reference(field, start):
    flat = field.reshape(NX, NZ * NY)
    gram_x = jnp.dot(flat.astype(jnp.float32), flat.T.astype(jnp.float32), precision=lax.Precision.HIGHEST, preferred_element_type=jnp.float32) / (NY * NZ)
    basis = start
    for step in range(ITERS):
        basis = orthonormal(jnp.dot(gram_x.astype(jnp.float32), basis.astype(jnp.float32), precision=lax.Precision.HIGHEST, preferred_element_type=jnp.float32))
    core = jnp.dot(basis.T.astype(jnp.float32), flat.astype(jnp.float32), precision=lax.Precision.HIGHEST, preferred_element_type=jnp.float32)
    core = core.reshape(RANK * NZ, NY)
    gram_y = jnp.dot(core.T.astype(jnp.float32), core.astype(jnp.float32), precision=lax.Precision.HIGHEST, preferred_element_type=jnp.float32) / (RANK * NZ)
    return (basis, gram_y)
```

```python
import functools

import jax
import jax.numpy as jnp
from jax import lax
from jax.experimental import pallas as pl
from jax.experimental.pallas import tpu as pltpu
from jax.sharding import PartitionSpec as P

ITERS = 4
CHUNKS = 4
WINDOW = 5
LINE = 4
MIB = 1024 * 1024
F32 = jnp.float32
BF16 = jnp.bfloat16


def halves(value):
    high = value.astype(BF16)
    low = (value - high.astype(F32)).astype(BF16)
    return high, low


def dot_nt(left, right):
    return lax.dot_general(left, right, (((1,), (1,)), ((), ())), preferred_element_type=F32)


def dot_tn(left, right):
    return lax.dot_general(left, right, (((0,), (0,)), ((), ())), preferred_element_type=F32)


def gram_body(steps, slab_ref, before_ref, out_ref, main, cross):
    step = pl.program_id(0)

    @pl.when(step == 0)
    def _():
        main[...] = jnp.zeros_like(main)
        cross[...] = jnp.zeros_like(cross)

    depth = slab_ref.shape[0]
    parts = [halves(slab_ref[z]) for z in range(depth)]
    high = jnp.concatenate([part[0] for part in parts], axis=1)
    low = jnp.concatenate([part[1] for part in parts], axis=1)
    main[...] += dot_nt(high, high)
    cross[...] += dot_nt(high, low)

    @pl.when(step == steps - 1)
    def _():
        mixed = cross[...]
        out_ref[...] = before_ref[...] + main[...] + mixed + mixed.T


def gram_of(slab, before):
    depth, width_x, width_y = slab.shape
    block = 4 if depth % 4 == 0 else 1
    steps = depth // block
    square = pl.BlockSpec((width_x, width_x), lambda i: (0, 0))
    return pl.pallas_call(
        functools.partial(gram_body, steps),
        grid=(steps,),
        in_specs=[pl.BlockSpec((block, width_x, width_y), lambda i: (i, 0, 0)), square],
        out_specs=square,
        out_shape=jax.ShapeDtypeStruct((width_x, width_x), F32),
        scratch_shapes=[pltpu.VMEM((width_x, width_x), F32)] * 2,
        compiler_params=pltpu.CompilerParams(vmem_limit_bytes=32 * MIB),
        cost_estimate=pl.CostEstimate(
            flops=4 * width_x * width_x * depth * width_y,
            bytes_accessed=slab.size * 4,
            transcendentals=0,
        ),
        name="gram_x",
    )(slab, before)


def core_body(steps, field_ref, basis_ref, out_ref, stacked_ref, high_ref, low_ref, main, cross):
    step = pl.program_id(0)
    rank = basis_ref.shape[1]

    @pl.when(step == 0)
    def _():
        main[...] = jnp.zeros_like(main)
        cross[...] = jnp.zeros_like(cross)
        basis_high, basis_low = halves(basis_ref[...].T)
        stacked_ref[:rank] = basis_high
        stacked_ref[rank:] = basis_low

    depth, blocks, _, width = field_ref.shape
    stacked = stacked_ref[...]
    for z in range(depth):
        for b in range(blocks):
            high, low = halves(field_ref[z, b])
            both = jnp.dot(stacked, high, preferred_element_type=F32)
            core = both[:rank] + both[rank:]
            core += jnp.dot(stacked[:rank], low, preferred_element_type=F32)
            core_high, core_low = halves(core)
            high_ref[pl.ds(z * rank, rank), pl.ds(b * width, width)] = core_high
            low_ref[pl.ds(z * rank, rank), pl.ds(b * width, width)] = core_low
    high = high_ref[...]
    main[...] += dot_tn(high, high)
    cross[...] += dot_tn(high, low_ref[...])

    @pl.when(step == steps - 1)
    def _():
        mixed = cross[...]
        out_ref[...] = main[...] + mixed + mixed.T


def core_gram(cells, basis):
    depth, blocks, width_x, width = cells.shape
    rank = basis.shape[1]
    width_y = blocks * width
    block = 2 if depth % 2 == 0 else 1
    steps = depth // block
    return pl.pallas_call(
        functools.partial(core_body, steps),
        grid=(steps,),
        in_specs=[
            pl.BlockSpec((block, blocks, width_x, width), lambda i: (i, 0, 0, 0)),
            pl.BlockSpec((width_x, rank), lambda i: (0, 0)),
        ],
        out_specs=pl.BlockSpec((width_y, width_y), lambda i: (0, 0)),
        out_shape=jax.ShapeDtypeStruct((width_y, width_y), F32),
        scratch_shapes=[
            pltpu.VMEM((2 * rank, width_x), BF16),
            pltpu.VMEM((block * rank, width_y), BF16),
            pltpu.VMEM((block * rank, width_y), BF16),
            pltpu.VMEM((width_y, width_y), F32),
            pltpu.VMEM((width_y, width_y), F32),
        ],
        compiler_params=pltpu.CompilerParams(vmem_limit_bytes=48 * MIB),
        cost_estimate=pl.CostEstimate(
            flops=6 * rank * cells.size + 4 * rank * depth * width_y * width_y,
            bytes_accessed=cells.size * 4,
            transcendentals=0,
        ),
        name="core_gram_y",
    )(cells, basis)


def full_dot(left, right, contract):
    return lax.dot_general(
        left,
        right,
        ((contract[:1], contract[1:]), ((), ())),
        precision=lax.Precision.HIGHEST,
        preferred_element_type=F32,
    )


def inverse_factor(cross):
    size = cross.shape[0]
    tall = 8
    wide = 4
    groups = size // tall
    shape = (tall, size)
    sublane = lax.broadcasted_iota(jnp.int32, shape, 0)
    lane = lax.broadcasted_iota(jnp.int32, shape, 1)
    left = [cross[t * tall : (t + 1) * tall] for t in range(groups)]
    right = [(lane == sublane + t * tall).astype(F32) for t in range(groups)]
    pivots = [jnp.ones(shape, F32) for _ in range(groups)]

    def row(value, s):
        return jnp.broadcast_to(value[s : s + 1, :], shape)

    for first in range(0, size, wide):
        top, s0 = first // tall, first % tall
        below = range(top, groups)
        columns = [
            {t: jnp.broadcast_to(left[t][:, first + k : first + k + 1], shape) for t in below}
            for k in range(wide)
        ]
        rows = [row(left[top], s0 + k) for k in range(wide)]
        eyes = [row(right[top], s0 + k) for k in range(wide)]
        scaled = []
        for i in range(wide):
            pivot = row(columns[i][top], s0 + i)
            inverse = 1.0 / pivot
            scaled.append((rows[i] * inverse, eyes[i] * inverse))
            for k in range(i + 1, wide):
                ratio = row(columns[i][top], s0 + k) * inverse
                for t in below:
                    columns[k][t] = columns[k][t] - ratio * columns[i][t]
                rows[k] = rows[k] - ratio * rows[i]
                eyes[k] = eyes[k] - ratio * eyes[i]
            here = sublane == s0 + i
            pivots[top] = jnp.where(here, pivot, pivots[top])
        rest = sublane >= s0 + wide
        for t in below:
            new_left, new_right = left[t], right[t]
            for i in range(wide):
                new_left = new_left - columns[i][t] * scaled[i][0]
                new_right = new_right - columns[i][t] * scaled[i][1]
            if t == top:
                new_left = jnp.where(rest, new_left, left[t])
                new_right = jnp.where(rest, new_right, right[t])
                for i in range(wide):
                    new_right = jnp.where(sublane == s0 + i, eyes[i], new_right)
            left[t], right[t] = new_left, new_right
    for t in range(groups):
        root = lax.rsqrt(pivots[t])
        root = root * (1.5 - 0.5 * pivots[t] * root * root)
        right[t] = right[t] * root
    return jnp.concatenate(right, axis=0)


def iterate_body(total, gram_ref, start_ref, out_ref, gram):
    gram[...] = gram_ref[...] / total
    out_ref[...] = start_ref[...]

    def step(_, carry):
        product = full_dot(gram[...], out_ref[...], (1, 0))
        inverse = inverse_factor(full_dot(product, product, (0, 0)))
        out_ref[...] = full_dot(product, inverse, (1, 1))
        return carry

    lax.fori_loop(0, ITERS, step, 0)


def iterate(gram_sum, start, total):
    width_x, rank = start.shape
    return pl.pallas_call(
        functools.partial(iterate_body, total),
        in_specs=[pl.BlockSpec(memory_space=pltpu.VMEM)] * 2,
        out_specs=pl.BlockSpec(memory_space=pltpu.VMEM),
        out_shape=jax.ShapeDtypeStruct((width_x, rank), F32),
        scratch_shapes=[pltpu.VMEM((width_x, width_x), F32)],
        compiler_params=pltpu.CompilerParams(vmem_limit_bytes=24 * MIB),
        name="subspace",
    )(gram_sum, start)


class Line:
    def __init__(self):
        self.ends = []

    def tied(self, value):
        if len(self.ends) >= WINDOW:
            value, _ = lax.optimization_barrier((value, self.ends[-WINDOW]))
        return value

    def send(self, value, axis, perm):
        got = lax.ppermute(value, axis, perm)
        self.ends.append(got)
        return got


def on_device(field, start):
    n = lax.axis_size("gx")
    m = lax.axis_size("yz")
    g = lax.axis_index("gx")
    q = lax.axis_index("yz")
    x_block, depth, y_block = field.shape
    width_x, width_y = x_block * n, y_block * m
    rank = start.shape[1]
    slab = depth // n
    chunks = CHUNKS if slab % (CHUNKS * m) == 0 else 1
    zc = slab // chunks
    zs = zc // m
    line = LINE if n % LINE == 0 else 1
    rest = n // line
    far = sorted(range(1, line), key=lambda a: abs(2 * a - line))
    shifts = [(a, b) for b in range(rest) for a in far] + [(0, b) for b in range(1, rest)]
    order = Line()

    def moved(index, a, b, sign):
        return (index // rest + sign * a) % line * rest + (index % rest + sign * b) % rest

    def gx_perm(a, b):
        return [(i, moved(i, a, b, 1)) for i in range(n)]

    state = {"cells": jnp.zeros((chunks * zs, m, width_x, y_block), F32), "cut": None}

    def to_gx(c, a, b, whole):
        source = order.tied(field)
        if len(order.ends) < WINDOW and state["cut"] is not None:
            source, _ = lax.optimization_barrier((field, state["cut"]))
        target = moved(g, a, b, 1)
        cut = lax.dynamic_slice_in_dim(source, target * slab + c * zc, zc, axis=1)
        cut = jnp.swapaxes(cut, 0, 1)
        state["cut"] = cut
        got = order.send(cut, "gx", gx_perm(a, b))
        return lax.dynamic_update_slice_in_dim(whole, got[:, None], moved(g, a, b, -1), axis=1)

    def to_yz(c, d, whole):
        cut = lax.dynamic_slice_in_dim(order.tied(whole), (q + d) % m * zs, zs, axis=0)
        got = order.send(cut, "yz", [(i, (i + d) % m) for i in range(m)])
        place = (c * zs, (q - d) % m, 0, 0)
        state["cells"] = lax.dynamic_update_slice(state["cells"], got[:, None], place)

    def keep_own(c, whole):
        own = lax.dynamic_slice_in_dim(whole, q * zs, zs, axis=0)
        state["cells"] = lax.dynamic_update_slice(state["cells"], own[:, None], (c * zs, q, 0, 0))

    gram_x = jnp.zeros((width_x, width_x), F32)
    before = None
    for c in range(chunks):
        whole = jnp.zeros((zc, n, x_block, y_block), F32)
        waiting = list(range(1, m)) if c else []
        for k, (a, b) in enumerate(shifts):
            whole = to_gx(c, a, b, whole)
            while waiting and (k + 1 == len(shifts) or k - 3 >= m - 1 - len(waiting)):
                to_yz(c - 1, waiting.pop(0), before)
                if k + 1 < len(shifts):
                    break
        own = lax.dynamic_slice_in_dim(field, g * slab + c * zc, zc, axis=1)
        own = jnp.swapaxes(own, 0, 1)[:, None]
        whole = lax.dynamic_update_slice_in_dim(whole, own, g, axis=1)
        before = whole.reshape(zc, width_x, y_block)
        gram_x = gram_of(before, gram_x)
        keep_own(c, before)
    for d in range(1, m):
        to_yz(chunks - 1, d, before)

    gram_x = lax.psum(gram_x, ("gx", "yz"))
    basis = iterate(gram_x, start, float(width_y * depth))
    partial_y = core_gram(state["cells"], basis) / float(rank * depth)
    rows_y = lax.psum_scatter(partial_y, "yz", scatter_dimension=0, tiled=True)
    width = width_y // n

    def block(index):
        return lax.dynamic_slice_in_dim(rows_y, index * width, width, axis=1)

    gram_y = block(g)
    for a, b in shifts:
        gram_y = gram_y + lax.ppermute(block(moved(g, a, b, 1)), "gx", gx_perm(a, b))
    return (basis, gram_y)


def solution(mesh):
    placed = (P("gx", None, "yz"), P())
    return jax.shard_map(
        on_device, mesh=mesh, in_specs=placed, out_specs=(P(), P("yz", "gx")), check_vma=False
    )
```

```python
import functools

import jax
import jax.numpy as jnp
from jax import lax
from jax.experimental import pallas as pl
from jax.experimental.pallas import tpu as pltpu
from jax.sharding import PartitionSpec as P

ITERS = 4
CHUNKS = 4
WINDOW = 5
LINE = 4
MIB = 1024 * 1024
F32 = jnp.float32
BF16 = jnp.bfloat16


def halves(value):
    high = value.astype(BF16)
    low = (value - high.astype(F32)).astype(BF16)
    return high, low


def dot_nt(left, right):
    return lax.dot_general(left, right, (((1,), (1,)), ((), ())), preferred_element_type=F32)


def dot_tn(left, right):
    return lax.dot_general(left, right, (((0,), (0,)), ((), ())), preferred_element_type=F32)


def gram_body(steps, slab_ref, before_ref, out_ref, main, cross):
    step = pl.program_id(0)

    @pl.when(step == 0)
    def _():
        main[...] = jnp.zeros_like(main)
        cross[...] = jnp.zeros_like(cross)

    depth = slab_ref.shape[0]
    parts = [halves(slab_ref[z]) for z in range(depth)]
    high = jnp.concatenate([part[0] for part in parts], axis=1)
    low = jnp.concatenate([part[1] for part in parts], axis=1)
    main[...] += dot_nt(high, high)
    cross[...] += dot_nt(high, low)

    @pl.when(step == steps - 1)
    def _():
        mixed = cross[...]
        out_ref[...] = before_ref[...] + main[...] + mixed + mixed.T


def gram_of(slab, before):
    depth, width_x, width_y = slab.shape
    block = 4 if depth % 4 == 0 else 1
    steps = depth // block
    square = pl.BlockSpec((width_x, width_x), lambda i: (0, 0))
    return pl.pallas_call(
        functools.partial(gram_body, steps),
        grid=(steps,),
        in_specs=[pl.BlockSpec((block, width_x, width_y), lambda i: (i, 0, 0)), square],
        out_specs=square,
        out_shape=jax.ShapeDtypeStruct((width_x, width_x), F32),
        scratch_shapes=[pltpu.VMEM((width_x, width_x), F32)] * 2,
        compiler_params=pltpu.CompilerParams(vmem_limit_bytes=32 * MIB),
        cost_estimate=pl.CostEstimate(
            flops=4 * width_x * width_x * depth * width_y,
            bytes_accessed=slab.size * 4,
            transcendentals=0,
        ),
        name="gram_x",
    )(slab, before)


def core_body(steps, total, field_ref, basis_ref, out_ref, stacked_ref, high_ref, low_ref, main, cross):
    step = pl.program_id(0)
    rank = basis_ref.shape[1]

    @pl.when(step == 0)
    def _():
        main[...] = jnp.zeros_like(main)
        cross[...] = jnp.zeros_like(cross)
        basis_high, basis_low = halves(basis_ref[...].T)
        stacked_ref[:rank] = basis_high
        stacked_ref[rank:] = basis_low

    depth, blocks, _, width = field_ref.shape
    stacked = stacked_ref[...]
    for z in range(depth):
        for b in range(blocks):
            high, low = halves(field_ref[z, b])
            both = jnp.dot(stacked, high, preferred_element_type=F32)
            core = both[:rank] + both[rank:]
            core += jnp.dot(stacked[:rank], low, preferred_element_type=F32)
            core_high, core_low = halves(core)
            high_ref[pl.ds(z * rank, rank), pl.ds(b * width, width)] = core_high
            low_ref[pl.ds(z * rank, rank), pl.ds(b * width, width)] = core_low
    high = high_ref[...]
    main[...] += dot_tn(high, high)
    cross[...] += dot_tn(high, low_ref[...])

    @pl.when(step == steps - 1)
    def _():
        mixed = cross[...]
        out_ref[...] = (main[...] + mixed + mixed.T) / total


def core_gram(cells, basis, total):
    depth, blocks, width_x, width = cells.shape
    rank = basis.shape[1]
    width_y = blocks * width
    block = 2 if depth % 2 == 0 else 1
    steps = depth // block
    return pl.pallas_call(
        functools.partial(core_body, steps, total),
        grid=(steps,),
        in_specs=[
            pl.BlockSpec((block, blocks, width_x, width), lambda i: (i, 0, 0, 0)),
            pl.BlockSpec((width_x, rank), lambda i: (0, 0)),
        ],
        out_specs=pl.BlockSpec((width_y, width_y), lambda i: (0, 0)),
        out_shape=jax.ShapeDtypeStruct((width_y, width_y), F32),
        scratch_shapes=[
            pltpu.VMEM((2 * rank, width_x), BF16),
            pltpu.VMEM((block * rank, width_y), BF16),
            pltpu.VMEM((block * rank, width_y), BF16),
            pltpu.VMEM((width_y, width_y), F32),
            pltpu.VMEM((width_y, width_y), F32),
        ],
        compiler_params=pltpu.CompilerParams(vmem_limit_bytes=48 * MIB),
        cost_estimate=pl.CostEstimate(
            flops=6 * rank * cells.size + 4 * rank * depth * width_y * width_y,
            bytes_accessed=cells.size * 4,
            transcendentals=0,
        ),
        name="core_gram_y",
    )(cells, basis)


def full_dot(left, right, contract):
    return lax.dot_general(
        left,
        right,
        ((contract[:1], contract[1:]), ((), ())),
        precision=lax.Precision.HIGHEST,
        preferred_element_type=F32,
    )


def inverse_factor(cross):
    size = cross.shape[0]
    tall = 8
    wide = 4
    groups = size // tall
    shape = (tall, size)
    sublane = lax.broadcasted_iota(jnp.int32, shape, 0)
    lane = lax.broadcasted_iota(jnp.int32, shape, 1)
    left = [cross[t * tall : (t + 1) * tall] for t in range(groups)]
    right = [(lane == sublane + t * tall).astype(F32) for t in range(groups)]
    pivots = [jnp.ones(shape, F32) for _ in range(groups)]

    def row(value, s):
        return jnp.broadcast_to(value[s : s + 1, :], shape)

    for first in range(0, size, wide):
        top, s0 = first // tall, first % tall
        below = range(top, groups)
        columns = [
            {t: jnp.broadcast_to(left[t][:, first + k : first + k + 1], shape) for t in below}
            for k in range(wide)
        ]
        rows = [row(left[top], s0 + k) for k in range(wide)]
        eyes = [row(right[top], s0 + k) for k in range(wide)]
        scaled = []
        for i in range(wide):
            pivot = row(columns[i][top], s0 + i)
            inverse = 1.0 / pivot
            scaled.append((rows[i] * inverse, eyes[i] * inverse))
            for k in range(i + 1, wide):
                ratio = row(columns[i][top], s0 + k) * inverse
                for t in below:
                    columns[k][t] = columns[k][t] - ratio * columns[i][t]
                rows[k] = rows[k] - ratio * rows[i]
                eyes[k] = eyes[k] - ratio * eyes[i]
            here = sublane == s0 + i
            pivots[top] = jnp.where(here, pivot, pivots[top])
        rest = sublane >= s0 + wide
        for t in below:
            new_left, new_right = left[t], right[t]
            for i in range(wide):
                new_left = new_left - columns[i][t] * scaled[i][0]
                new_right = new_right - columns[i][t] * scaled[i][1]
            if t == top:
                new_left = jnp.where(rest, new_left, left[t])
                new_right = jnp.where(rest, new_right, right[t])
                for i in range(wide):
                    new_right = jnp.where(sublane == s0 + i, eyes[i], new_right)
            left[t], right[t] = new_left, new_right
    for t in range(groups):
        root = lax.rsqrt(pivots[t])
        root = root * (1.5 - 0.5 * pivots[t] * root * root)
        right[t] = right[t] * root
    return jnp.concatenate(right, axis=0)


def iterate_body(total, places_ref, *refs):
    *piece_refs, start_ref, out_ref, gram = refs
    height = piece_refs[0].shape[0]
    for i, piece_ref in enumerate(piece_refs):
        place = pl.multiple_of(places_ref[i] * height, height)
        gram[pl.ds(place, height)] = piece_ref[...] / total
    out_ref[...] = start_ref[...]

    def step(_, carry):
        product = full_dot(gram[...], out_ref[...], (1, 0))
        inverse = inverse_factor(full_dot(product, product, (0, 0)))
        out_ref[...] = full_dot(product, inverse, (1, 1))
        return carry

    lax.fori_loop(0, ITERS, step, 0)


def iterate(pieces, places, start, total):
    width_x, rank = start.shape
    return pl.pallas_call(
        functools.partial(iterate_body, total),
        in_specs=[pl.BlockSpec(memory_space=pltpu.SMEM)]
        + [pl.BlockSpec(memory_space=pltpu.VMEM)] * (len(pieces) + 1),
        out_specs=pl.BlockSpec(memory_space=pltpu.VMEM),
        out_shape=jax.ShapeDtypeStruct((width_x, rank), F32),
        scratch_shapes=[pltpu.VMEM((width_x, width_x), F32)],
        compiler_params=pltpu.CompilerParams(vmem_limit_bytes=24 * MIB),
        name="subspace",
    )(places, *pieces, start)


def stack_body(places_ref, *refs):
    *piece_refs, out_ref = refs
    for i, piece_ref in enumerate(piece_refs):
        out_ref[places_ref[i]] = piece_ref[...]


def stack(pieces, places):
    return pl.pallas_call(
        stack_body,
        in_specs=[pl.BlockSpec(memory_space=pltpu.SMEM)]
        + [pl.BlockSpec(memory_space=pltpu.VMEM)] * len(pieces),
        out_specs=pl.BlockSpec(memory_space=pltpu.VMEM),
        out_shape=jax.ShapeDtypeStruct((len(pieces),) + pieces[0].shape, F32),
        compiler_params=pltpu.CompilerParams(vmem_limit_bytes=16 * MIB),
        name="stack_rows",
    )(places, *pieces)


def tie(value, others):
    return lax.optimization_barrier((value, *others))[0] if others else value


class Line:
    def __init__(self):
        self.ends = []

    def done(self, ahead):
        last = len(self.ends) - WINDOW + 1 - ahead
        return self.ends[max(0, last - WINDOW) : max(0, last)]

    def send(self, cut, source, axis, perm):
        value = cut(tie(source, self.done(2)))
        got = lax.ppermute(tie(value, self.done(0)), axis, perm)
        self.ends.append(got)
        return got


def chunk_depths(units):
    last = max(1, units // 8)
    others = min(CHUNKS - 1, units - last)
    return [(units - last + k) // others for k in reversed(range(others))] + [last]


def on_device(field, start):
    n = lax.axis_size("gx")
    m = lax.axis_size("yz")
    g = lax.axis_index("gx")
    q = lax.axis_index("yz")
    x_block, depth, y_block = field.shape
    width_x, width_y = x_block * n, y_block * m
    rank = start.shape[1]
    slab = depth // n
    line = LINE if n % LINE == 0 else 1
    rest = n // line
    order = Line()

    def moved(index, a, b, sign=1):
        return (index // rest + sign * a) % line * rest + (index % rest + sign * b) % rest

    def gx_perm(a, b):
        return [(i, moved(i, a, b)) for i in range(n)]

    def yz_perm(d):
        return [(i, (i + d) % m) for i in range(m)]

    far = sorted(range(1, line), key=lambda a: abs(2 * a - line))
    shifts = [(a, (b + k) % rest) for b in range(rest) for k, a in enumerate(far)]
    shifts[4:4] = [(0, b) for b in range(1, rest)]
    turns = sorted(range(1, m), key=lambda d: abs(2 * d - m))

    cells = jnp.zeros((slab // m, m, width_x, y_block), F32)

    def to_gx(first, zc, a, b, whole):
        def cut(source):
            place = moved(g, a, b) * slab + first
            return jnp.swapaxes(lax.dynamic_slice_in_dim(source, place, zc, axis=1), 0, 1)

        got = order.send(cut, field, "gx", gx_perm(a, b))
        return lax.dynamic_update_slice_in_dim(whole, got[:, None], moved(g, a, b, -1), axis=1)

    def to_yz(cells, first, d, whole):
        zs = whole.shape[0] // m

        def cut(source):
            return lax.dynamic_slice_in_dim(source, (q + d) % m * zs, zs, axis=0)

        got = order.send(cut, whole, "yz", yz_perm(d))
        return lax.dynamic_update_slice(cells, got[:, None], (first // m, (q - d) % m, 0, 0))

    gram = jnp.zeros((width_x, width_x), F32)
    before, start_z, first = None, 0, 0
    for units in chunk_depths(slab // m):
        zc = units * m
        whole = jnp.zeros((zc, n, x_block, y_block), F32)
        waiting = list(turns) if before is not None else []
        for k, (a, b) in enumerate(shifts):
            whole = to_gx(first, zc, a, b, whole)
            if k >= WINDOW - 1 and waiting:
                cells = to_yz(cells, start_z, waiting.pop(0), before)
        for d in waiting:
            cells = to_yz(cells, start_z, d, before)
        own = lax.dynamic_slice_in_dim(field, g * slab + first, zc, axis=1)
        own = jnp.swapaxes(own, 0, 1)[:, None]
        whole = lax.dynamic_update_slice_in_dim(whole, own, g, axis=1)
        before = whole.reshape(zc, width_x, y_block)
        gram = gram_of(before, gram)
        own = lax.dynamic_slice_in_dim(before, q * units, units, axis=0)
        cells = lax.dynamic_update_slice(cells, own[:, None], (first // m, q, 0, 0))
        start_z, first = first, first + zc

    rows = width_x // m
    slabs = gram.reshape(m, rows, width_x)

    def pick(array, index):
        return lax.dynamic_index_in_dim(array, index, axis=0, keepdims=False)

    summed = pick(slabs, q)
    for d in turns:
        summed = summed + lax.ppermute(pick(slabs, (q + d) % m), "yz", yz_perm(d))
    before = tie(before, [summed])
    cells = to_yz(cells, start_z, turns[0], before)
    strips = summed.reshape(n, rows // n, width_x)
    summed = pick(strips, g)
    for a, b in shifts:
        summed = summed + lax.ppermute(pick(strips, moved(g, a, b)), "gx", gx_perm(a, b))
    before = tie(before, [summed])
    for d in turns[1:]:
        cells = to_yz(cells, start_z, d, before)
    pieces = [summed] + [lax.ppermute(summed, "gx", gx_perm(a, b)) for a, b in shifts]
    places = jnp.stack([g] + [moved(g, a, b, -1) for a, b in shifts]).astype(jnp.int32)
    summed = stack(pieces, places).reshape(rows, width_x)
    pieces = [summed] + [lax.ppermute(summed, "yz", yz_perm(d)) for d in turns]
    places = jnp.stack([q] + [(q - d) % m for d in turns]).astype(jnp.int32)
    basis = iterate(pieces, places, start, float(width_y * depth))

    partial_y = core_gram(cells, basis, float(rank * depth))
    cores = 2 if m % 2 == 0 else 1
    chips = m // cores
    core, chip = q % cores, q // cores
    blocks = partial_y.reshape(chips, cores, y_block, width_y)

    def of_core(index):
        return lax.dynamic_index_in_dim(blocks, index, axis=1, keepdims=False)

    blocks_here = of_core(core)
    for d in range(1, cores):
        perm = [(i, i // cores * cores + (i + d) % cores) for i in range(m)]
        blocks_here = blocks_here + lax.ppermute(of_core((core + d) % cores), "yz", perm)
    rows_y = pick(blocks_here, chip)
    for d in range(1, chips):
        perm = [(i, (i + d * cores) % m) for i in range(m)]
        rows_y = rows_y + lax.ppermute(pick(blocks_here, (chip + d) % chips), "yz", perm)
    width = width_y // n

    def block(index):
        return lax.dynamic_slice_in_dim(rows_y, index * width, width, axis=1)

    gram_y = block(g)
    for a, b in shifts:
        gram_y = gram_y + lax.ppermute(block(moved(g, a, b)), "gx", gx_perm(a, b))
    return (basis, gram_y)


def solution(mesh):
    placed = (P("gx", None, "yz"), P())
    return jax.shard_map(
        on_device, mesh=mesh, in_specs=placed, out_specs=(P(), P("yz", "gx")), check_vma=False
    )
```

```python
import functools
import math

import jax
import jax.numpy as jnp
from jax import lax
from jax.experimental import pallas as pl
from jax.experimental.pallas import tpu as pltpu
from jax.sharding import PartitionSpec as P

ITERS = 4
WINDOW = 5
TALL = 8
LINE = 4
MIB = 1024 * 1024
F32 = jnp.float32
BF16 = jnp.bfloat16


def halves(value):
    high = value.astype(BF16)
    low = (value - high.astype(F32)).astype(BF16)
    return high, low


def dot_nt(left, right):
    return lax.dot_general(left, right, (((1,), (1,)), ((), ())), preferred_element_type=F32)


def dot_tn(left, right):
    return lax.dot_general(left, right, (((0,), (0,)), ((), ())), preferred_element_type=F32)


def gram_body(steps, slab_ref, before_ref, out_ref, main, cross):
    step = pl.program_id(0)

    @pl.when(step == 0)
    def _():
        main[...] = jnp.zeros_like(main)
        cross[...] = jnp.zeros_like(cross)

    depth = slab_ref.shape[0]
    parts = [halves(slab_ref[z]) for z in range(depth)]
    high = jnp.concatenate([part[0] for part in parts], axis=1)
    low = jnp.concatenate([part[1] for part in parts], axis=1)
    main[...] += dot_nt(high, high)
    cross[...] += dot_nt(high, low)

    @pl.when(step == steps - 1)
    def _():
        mixed = cross[...]
        out_ref[...] = before_ref[...] + main[...] + mixed + mixed.T


def gram_of(slab, before):
    depth, width_x, width_y = slab.shape
    block = 4 if depth % 4 == 0 else 1
    steps = depth // block
    square = pl.BlockSpec((width_x, width_x), lambda i: (0, 0))
    return pl.pallas_call(
        functools.partial(gram_body, steps),
        grid=(steps,),
        in_specs=[pl.BlockSpec((block, width_x, width_y), lambda i: (i, 0, 0)), square],
        out_specs=square,
        out_shape=jax.ShapeDtypeStruct((width_x, width_x), F32),
        scratch_shapes=[pltpu.VMEM((width_x, width_x), F32)] * 2,
        compiler_params=pltpu.CompilerParams(vmem_limit_bytes=32 * MIB),
        cost_estimate=pl.CostEstimate(
            flops=4 * width_x * width_x * depth * width_y,
            bytes_accessed=slab.size * 4,
            transcendentals=0,
        ),
        name="gram_x",
    )(slab, before)


def core_body(steps, total, field_ref, basis_ref, out_ref, stacked_ref, high_ref, low_ref, main, cross):
    step = pl.program_id(0)
    rank = basis_ref.shape[1]

    @pl.when(step == 0)
    def _():
        main[...] = jnp.zeros_like(main)
        cross[...] = jnp.zeros_like(cross)
        basis_high, basis_low = halves(basis_ref[...].T)
        stacked_ref[:rank] = basis_high
        stacked_ref[rank:] = basis_low

    depth, blocks, _, width = field_ref.shape
    stacked = stacked_ref[...]
    for z in range(depth):
        for b in range(blocks):
            high, low = halves(field_ref[z, b])
            both = jnp.dot(stacked, high, preferred_element_type=F32)
            core = both[:rank] + both[rank:]
            core += jnp.dot(stacked[:rank], low, preferred_element_type=F32)
            core_high, core_low = halves(core)
            high_ref[pl.ds(z * rank, rank), pl.ds(b * width, width)] = core_high
            low_ref[pl.ds(z * rank, rank), pl.ds(b * width, width)] = core_low
    high = high_ref[...]
    main[...] += dot_tn(high, high)
    cross[...] += dot_tn(high, low_ref[...])

    @pl.when(step == steps - 1)
    def _():
        mixed = cross[...]
        out_ref[...] = (main[...] + mixed + mixed.T) / total


def core_gram(cells, basis, total):
    depth, blocks, width_x, width = cells.shape
    rank = basis.shape[1]
    width_y = blocks * width
    block = 2 if depth % 2 == 0 else 1
    steps = depth // block
    return pl.pallas_call(
        functools.partial(core_body, steps, total),
        grid=(steps,),
        in_specs=[
            pl.BlockSpec((block, blocks, width_x, width), lambda i: (i, 0, 0, 0)),
            pl.BlockSpec((width_x, rank), lambda i: (0, 0)),
        ],
        out_specs=pl.BlockSpec((width_y, width_y), lambda i: (0, 0)),
        out_shape=jax.ShapeDtypeStruct((width_y, width_y), F32),
        scratch_shapes=[
            pltpu.VMEM((2 * rank, width_x), BF16),
            pltpu.VMEM((block * rank, width_y), BF16),
            pltpu.VMEM((block * rank, width_y), BF16),
            pltpu.VMEM((width_y, width_y), F32),
            pltpu.VMEM((width_y, width_y), F32),
        ],
        compiler_params=pltpu.CompilerParams(vmem_limit_bytes=48 * MIB),
        cost_estimate=pl.CostEstimate(
            flops=6 * rank * cells.size + 4 * rank * depth * width_y * width_y,
            bytes_accessed=cells.size * 4,
            transcendentals=0,
        ),
        name="core_gram_y",
    )(cells, basis)


def full_dot(left, right, contract):
    return lax.dot_general(
        left,
        right,
        ((contract[:1], contract[1:]), ((), ())),
        precision=lax.Precision.HIGHEST,
        preferred_element_type=F32,
    )


def inverse_factor(cross):
    size = cross.shape[0]
    tall = 8
    wide = 4
    groups = size // tall
    shape = (tall, size)
    sublane = lax.broadcasted_iota(jnp.int32, shape, 0)
    lane = lax.broadcasted_iota(jnp.int32, shape, 1)
    left = [cross[t * tall : (t + 1) * tall] for t in range(groups)]
    right = [(lane == sublane + t * tall).astype(F32) for t in range(groups)]
    pivots = [jnp.ones(shape, F32) for _ in range(groups)]

    def row(value, s):
        return jnp.broadcast_to(value[s : s + 1, :], shape)

    for first in range(0, size, wide):
        top, s0 = first // tall, first % tall
        below = range(top, groups)
        columns = [
            {t: jnp.broadcast_to(left[t][:, first + k : first + k + 1], shape) for t in below}
            for k in range(wide)
        ]
        rows = [row(left[top], s0 + k) for k in range(wide)]
        eyes = [row(right[top], s0 + k) for k in range(wide)]
        scaled = []
        for i in range(wide):
            pivot = row(columns[i][top], s0 + i)
            inverse = 1.0 / pivot
            scaled.append((rows[i] * inverse, eyes[i] * inverse))
            for k in range(i + 1, wide):
                ratio = row(columns[i][top], s0 + k) * inverse
                for t in below:
                    columns[k][t] = columns[k][t] - ratio * columns[i][t]
                rows[k] = rows[k] - ratio * rows[i]
                eyes[k] = eyes[k] - ratio * eyes[i]
            here = sublane == s0 + i
            pivots[top] = jnp.where(here, pivot, pivots[top])
        rest = sublane >= s0 + wide
        for t in below:
            new_left, new_right = left[t], right[t]
            for i in range(wide):
                new_left = new_left - columns[i][t] * scaled[i][0]
                new_right = new_right - columns[i][t] * scaled[i][1]
            if t == top:
                new_left = jnp.where(rest, new_left, left[t])
                new_right = jnp.where(rest, new_right, right[t])
                for i in range(wide):
                    new_right = jnp.where(sublane == s0 + i, eyes[i], new_right)
            left[t], right[t] = new_left, new_right
    for t in range(groups):
        root = lax.rsqrt(pivots[t])
        root = root * (1.5 - 0.5 * pivots[t] * root * root)
        right[t] = right[t] * root
    return jnp.concatenate(right, axis=0)


def iterate_body(total, places_ref, *refs):
    *piece_refs, start_ref, out_ref, gram = refs
    height = piece_refs[0].shape[0]
    for i, piece_ref in enumerate(piece_refs):
        place = pl.multiple_of(places_ref[i] * height, height)
        gram[pl.ds(place, height)] = piece_ref[...] / total
    out_ref[...] = start_ref[...]

    def step(_, carry):
        product = full_dot(gram[...], out_ref[...], (1, 0))
        inverse = inverse_factor(full_dot(product, product, (0, 0)))
        out_ref[...] = full_dot(product, inverse, (1, 1))
        return carry

    lax.fori_loop(0, ITERS, step, 0)


def iterate(pieces, places, start, total):
    width_x, rank = start.shape
    return pl.pallas_call(
        functools.partial(iterate_body, total),
        in_specs=[pl.BlockSpec(memory_space=pltpu.SMEM)]
        + [pl.BlockSpec(memory_space=pltpu.VMEM)] * (len(pieces) + 1),
        out_specs=pl.BlockSpec(memory_space=pltpu.VMEM),
        out_shape=jax.ShapeDtypeStruct((width_x, rank), F32),
        scratch_shapes=[pltpu.VMEM((width_x, width_x), F32)],
        compiler_params=pltpu.CompilerParams(vmem_limit_bytes=24 * MIB),
        cost_estimate=pl.CostEstimate(
            flops=4 * 10**10, bytes_accessed=8 * start.size, transcendentals=0
        ),
        name="subspace",
    )(places, *pieces, start)


def stack_body(places_ref, *refs):
    *piece_refs, out_ref = refs
    for i, piece_ref in enumerate(piece_refs):
        out_ref[places_ref[i]] = piece_ref[...]


def stack(pieces, places):
    return pl.pallas_call(
        stack_body,
        in_specs=[pl.BlockSpec(memory_space=pltpu.SMEM)]
        + [pl.BlockSpec(memory_space=pltpu.VMEM)] * len(pieces),
        out_specs=pl.BlockSpec(memory_space=pltpu.VMEM),
        out_shape=jax.ShapeDtypeStruct((len(pieces),) + pieces[0].shape, F32),
        compiler_params=pltpu.CompilerParams(vmem_limit_bytes=16 * MIB),
        name="stack_rows",
    )(places, *pieces)


def pack_body(first_ref, field_ref, out_ref):
    for z in range(field_ref.shape[1]):
        out_ref[z] = field_ref[:, z, :]


def pack(field, first, depth):
    x_block, _, y_block = field.shape
    return pl.pallas_call(
        pack_body,
        grid_spec=pltpu.PrefetchScalarGridSpec(
            num_scalar_prefetch=1,
            grid=(depth // TALL,),
            in_specs=[pl.BlockSpec((x_block, TALL, y_block), lambda i, at: (0, at[0] + i, 0))],
            out_specs=pl.BlockSpec((TALL, x_block, y_block), lambda i, at: (i, 0, 0)),
        ),
        out_shape=jax.ShapeDtypeStruct((depth, x_block, y_block), F32),
        compiler_params=pltpu.CompilerParams(vmem_limit_bytes=8 * MIB),
        cost_estimate=pl.CostEstimate(
            flops=0, bytes_accessed=8 * depth * x_block * y_block, transcendentals=0
        ),
        name="pack_z",
    )(first.astype(jnp.int32).reshape(1), field)


def tie(value, others):
    return lax.optimization_barrier((value, *others))[0] if others else value


class Line:
    def __init__(self):
        self.ends = []

    def done(self):
        last = len(self.ends) - WINDOW + 1
        return self.ends[max(0, last - 1) : max(0, last)]

    def send(self, cut, source, axis, perm):
        got = lax.ppermute(cut(tie(source, self.done())), axis, perm)
        self.ends.append(got)
        return got


def chunk_depths(groups):
    if groups < 4:
        return [groups]
    third, last = max(1, groups // 4), max(1, groups // 8)
    left = groups - third - last
    return [left - left // 2, left // 2, third, last]


def on_device(field, start):
    n = lax.axis_size("gx")
    m = lax.axis_size("yz")
    g = lax.axis_index("gx")
    q = lax.axis_index("yz")
    x_block, depth, y_block = field.shape
    width_x, width_y = x_block * n, y_block * m
    rank = start.shape[1]
    slab = depth // n
    line = LINE if n % LINE == 0 else 1
    rest = n // line
    order = Line()

    def moved(index, a, b, sign=1):
        return (index // rest + sign * a) % line * rest + (index % rest + sign * b) % rest

    def gx_perm(a, b):
        return [(i, moved(i, a, b)) for i in range(n)]

    def yz_perm(d):
        return [(i, (i + d) % m) for i in range(m)]

    far = sorted(range(1, line), key=lambda a: abs(2 * a - line))
    shifts = [(a, (b + k) % rest) for b in range(rest) for k, a in enumerate(far)]
    shifts[4:4] = [(0, b) for b in range(1, rest)]
    turns = sorted(range(1, m), key=lambda d: abs(2 * d - m))

    cells = jnp.zeros((slab // m, m, width_x, y_block), F32)

    def to_gx(first, zc, a, b, whole):
        place = (moved(g, a, b) * slab + first) // TALL
        got = order.send(lambda at: pack(field, at, zc), place, "gx", gx_perm(a, b))
        return lax.dynamic_update_slice_in_dim(whole, got[:, None], moved(g, a, b, -1), axis=1)

    def to_yz(cells, first, d, whole, after=()):
        zs = whole.shape[0] // m

        def cut(source):
            return lax.dynamic_slice_in_dim(source, (q + d) % m * zs, zs, axis=0)

        got = order.send(cut, tie(whole, after), "yz", yz_perm(d))
        return lax.dynamic_update_slice(cells, got[:, None], (first // m, (q - d) % m, 0, 0))

    gram = jnp.zeros((width_x, width_x), F32)
    before, start_z, first = None, 0, 0
    group = math.lcm(m, TALL)
    for groups in chunk_depths(slab // group):
        zc = groups * group
        units = zc // m
        whole = jnp.zeros((zc, n, x_block, y_block), F32)
        waiting = list(turns) if before is not None else []
        for k, (a, b) in enumerate(shifts):
            whole = to_gx(first, zc, a, b, whole)
            if k >= WINDOW - 1 and waiting:
                cells = to_yz(cells, start_z, waiting.pop(0), before)
        for d in waiting:
            cells = to_yz(cells, start_z, d, before)
        across = order.ends[-len(shifts) - len(turns) :]
        own = pack(field, (g * slab + first) // TALL, zc)[:, None]
        whole = lax.dynamic_update_slice_in_dim(whole, own, g, axis=1)
        before = whole.reshape(zc, width_x, y_block)
        gram = gram_of(before, gram)
        own = lax.dynamic_slice_in_dim(before, q * units, units, axis=0)
        cells = lax.dynamic_update_slice(cells, own[:, None], (first // m, q, 0, 0))
        start_z, first = first, first + zc

    rows = width_x // m
    slabs = tie(gram, across).reshape(m, rows, width_x)

    def pick(array, index):
        return lax.dynamic_index_in_dim(array, index, axis=0, keepdims=False)

    summed = pick(slabs, q)
    for d in turns:
        summed = summed + lax.ppermute(pick(slabs, (q + d) % m), "yz", yz_perm(d))
    cells = to_yz(cells, start_z, turns[0], before, [summed])
    strips = summed.reshape(n, rows // n, width_x)
    summed = pick(strips, g)
    for a, b in shifts:
        summed = summed + lax.ppermute(pick(strips, moved(g, a, b)), "gx", gx_perm(a, b))
    pieces = [summed] + [lax.ppermute(summed, "gx", gx_perm(a, b)) for a, b in shifts]
    places = jnp.stack([g] + [moved(g, a, b, -1) for a, b in shifts]).astype(jnp.int32)
    summed = stack(pieces, places).reshape(rows, width_x)
    pieces = [summed] + [lax.ppermute(summed, "yz", yz_perm(d)) for d in turns]
    places = jnp.stack([q] + [(q - d) % m for d in turns]).astype(jnp.int32)
    for d in turns[1:]:
        cells = to_yz(cells, start_z, d, before, pieces[1:])
    basis = iterate(pieces, places, start, float(width_y * depth))

    partial_y = core_gram(cells, basis, float(rank * depth))
    cores = 2 if m % 2 == 0 else 1
    chips = m // cores
    core, chip = q % cores, q // cores
    blocks = partial_y.reshape(chips, cores, y_block, width_y)

    def of_core(index):
        return lax.dynamic_index_in_dim(blocks, index, axis=1, keepdims=False)

    blocks_here = of_core(core)
    for d in range(1, cores):
        perm = [(i, i // cores * cores + (i + d) % cores) for i in range(m)]
        blocks_here = blocks_here + lax.ppermute(of_core((core + d) % cores), "yz", perm)
    rows_y = pick(blocks_here, chip)
    for d in range(1, chips):
        perm = [(i, (i + d * cores) % m) for i in range(m)]
        rows_y = rows_y + lax.ppermute(pick(blocks_here, (chip + d) % chips), "yz", perm)
    width = width_y // n

    def block(index):
        return lax.dynamic_slice_in_dim(rows_y, index * width, width, axis=1)

    gram_y = block(g)
    for a, b in shifts:
        gram_y = gram_y + lax.ppermute(block(moved(g, a, b)), "gx", gx_perm(a, b))
    return (basis, gram_y)


def solution(mesh):
    placed = (P("gx", None, "yz"), P())
    return jax.shard_map(
        on_device, mesh=mesh, in_specs=placed, out_specs=(P(), P("yz", "gx")), check_vma=False
    )
```

```python
import functools
import math

import jax
import jax.numpy as jnp
from jax import lax
from jax.experimental import pallas as pl
from jax.experimental.pallas import tpu as pltpu
from jax.sharding import PartitionSpec as P

ITERS = 4
WINDOW = 5
TALL = 8
LINE = 4
MIB = 1024 * 1024
F32 = jnp.float32
BF16 = jnp.bfloat16


def halves(value):
    high = value.astype(BF16)
    low = (value - high.astype(F32)).astype(BF16)
    return high, low


def dot_nt(left, right):
    return lax.dot_general(left, right, (((1,), (1,)), ((), ())), preferred_element_type=F32)


def dot_tn(left, right):
    return lax.dot_general(left, right, (((0,), (0,)), ((), ())), preferred_element_type=F32)


def gram_body(steps, slab_ref, before_ref, out_ref, main, cross):
    step = pl.program_id(0)

    @pl.when(step == 0)
    def _():
        main[...] = jnp.zeros_like(main)
        cross[...] = jnp.zeros_like(cross)

    depth = slab_ref.shape[0]
    parts = [halves(slab_ref[z]) for z in range(depth)]
    high = jnp.concatenate([part[0] for part in parts], axis=1)
    low = jnp.concatenate([part[1] for part in parts], axis=1)
    main[...] += dot_nt(high, high)
    cross[...] += dot_nt(high, low)

    @pl.when(step == steps - 1)
    def _():
        mixed = cross[...]
        out_ref[...] = before_ref[...] + main[...] + mixed + mixed.T


def gram_of(slab, before):
    depth, width_x, width_y = slab.shape
    block = 4 if depth % 4 == 0 else 1
    steps = depth // block
    square = pl.BlockSpec((width_x, width_x), lambda i: (0, 0))
    return pl.pallas_call(
        functools.partial(gram_body, steps),
        grid=(steps,),
        in_specs=[pl.BlockSpec((block, width_x, width_y), lambda i: (i, 0, 0)), square],
        out_specs=square,
        out_shape=jax.ShapeDtypeStruct((width_x, width_x), F32),
        scratch_shapes=[pltpu.VMEM((width_x, width_x), F32)] * 2,
        compiler_params=pltpu.CompilerParams(vmem_limit_bytes=32 * MIB),
        cost_estimate=pl.CostEstimate(
            flops=4 * width_x * width_x * depth * width_y,
            bytes_accessed=slab.size * 4,
            transcendentals=0,
        ),
        name="gram_x",
    )(slab, before)


def core_body(steps, total, field_ref, basis_ref, out_ref, stacked_ref, high_ref, low_ref, main, cross):
    step = pl.program_id(0)
    rank = basis_ref.shape[1]

    @pl.when(step == 0)
    def _():
        main[...] = jnp.zeros_like(main)
        cross[...] = jnp.zeros_like(cross)
        basis_high, basis_low = halves(basis_ref[...].T)
        stacked_ref[:rank] = basis_high
        stacked_ref[rank:] = basis_low

    depth, blocks, _, width = field_ref.shape
    stacked = stacked_ref[...]
    for z in range(depth):
        for b in range(blocks):
            high, low = halves(field_ref[z, b])
            both = jnp.dot(stacked, high, preferred_element_type=F32)
            core = both[:rank] + both[rank:]
            core += jnp.dot(stacked[:rank], low, preferred_element_type=F32)
            core_high, core_low = halves(core)
            high_ref[pl.ds(z * rank, rank), pl.ds(b * width, width)] = core_high
            low_ref[pl.ds(z * rank, rank), pl.ds(b * width, width)] = core_low
    high = high_ref[...]
    main[...] += dot_tn(high, high)
    cross[...] += dot_tn(high, low_ref[...])

    @pl.when(step == steps - 1)
    def _():
        mixed = cross[...]
        out_ref[...] = (main[...] + mixed + mixed.T) / total


def core_gram(cells, basis, total):
    depth, blocks, width_x, width = cells.shape
    rank = basis.shape[1]
    width_y = blocks * width
    block = 2 if depth % 2 == 0 else 1
    steps = depth // block
    return pl.pallas_call(
        functools.partial(core_body, steps, total),
        grid=(steps,),
        in_specs=[
            pl.BlockSpec((block, blocks, width_x, width), lambda i: (i, 0, 0, 0)),
            pl.BlockSpec((width_x, rank), lambda i: (0, 0)),
        ],
        out_specs=pl.BlockSpec((width_y, width_y), lambda i: (0, 0)),
        out_shape=jax.ShapeDtypeStruct((width_y, width_y), F32),
        scratch_shapes=[
            pltpu.VMEM((2 * rank, width_x), BF16),
            pltpu.VMEM((block * rank, width_y), BF16),
            pltpu.VMEM((block * rank, width_y), BF16),
            pltpu.VMEM((width_y, width_y), F32),
            pltpu.VMEM((width_y, width_y), F32),
        ],
        compiler_params=pltpu.CompilerParams(vmem_limit_bytes=48 * MIB),
        cost_estimate=pl.CostEstimate(
            flops=6 * rank * cells.size + 4 * rank * depth * width_y * width_y,
            bytes_accessed=cells.size * 4,
            transcendentals=0,
        ),
        name="core_gram_y",
    )(cells, basis)


def full_dot(left, right, contract):
    return lax.dot_general(
        left,
        right,
        ((contract[:1], contract[1:]), ((), ())),
        precision=lax.Precision.HIGHEST,
        preferred_element_type=F32,
    )


def inverse_factor(cross):
    size = cross.shape[0]
    tall = 8
    wide = 4
    groups = size // tall
    shape = (tall, size)
    sublane = lax.broadcasted_iota(jnp.int32, shape, 0)
    lane = lax.broadcasted_iota(jnp.int32, shape, 1)
    left = [cross[t * tall : (t + 1) * tall] for t in range(groups)]
    right = [(lane == sublane + t * tall).astype(F32) for t in range(groups)]
    pivots = [jnp.ones(shape, F32) for _ in range(groups)]

    def row(value, s):
        return jnp.broadcast_to(value[s : s + 1, :], shape)

    for first in range(0, size, wide):
        top, s0 = first // tall, first % tall
        below = range(top, groups)
        columns = [
            {t: jnp.broadcast_to(left[t][:, first + k : first + k + 1], shape) for t in below}
            for k in range(wide)
        ]
        rows = [row(left[top], s0 + k) for k in range(wide)]
        eyes = [row(right[top], s0 + k) for k in range(wide)]
        scaled = []
        for i in range(wide):
            pivot = row(columns[i][top], s0 + i)
            inverse = 1.0 / pivot
            scaled.append((rows[i] * inverse, eyes[i] * inverse))
            for k in range(i + 1, wide):
                ratio = row(columns[i][top], s0 + k) * inverse
                for t in below:
                    columns[k][t] = columns[k][t] - ratio * columns[i][t]
                rows[k] = rows[k] - ratio * rows[i]
                eyes[k] = eyes[k] - ratio * eyes[i]
            here = sublane == s0 + i
            pivots[top] = jnp.where(here, pivot, pivots[top])
        rest = sublane >= s0 + wide
        for t in below:
            new_left, new_right = left[t], right[t]
            for i in range(wide):
                new_left = new_left - columns[i][t] * scaled[i][0]
                new_right = new_right - columns[i][t] * scaled[i][1]
            if t == top:
                new_left = jnp.where(rest, new_left, left[t])
                new_right = jnp.where(rest, new_right, right[t])
                for i in range(wide):
                    new_right = jnp.where(sublane == s0 + i, eyes[i], new_right)
            left[t], right[t] = new_left, new_right
    for t in range(groups):
        root = lax.rsqrt(pivots[t])
        root = root * (1.5 - 0.5 * pivots[t] * root * root)
        right[t] = right[t] * root
    return jnp.concatenate(right, axis=0)


def iterate_body(total, places_ref, *refs):
    *piece_refs, start_ref, out_ref, gram = refs
    height = piece_refs[0].shape[0]
    for i, piece_ref in enumerate(piece_refs):
        place = pl.multiple_of(places_ref[i] * height, height)
        gram[pl.ds(place, height)] = piece_ref[...] / total
    out_ref[...] = start_ref[...]

    def step(_, carry):
        product = full_dot(gram[...], out_ref[...], (1, 0))
        inverse = inverse_factor(full_dot(product, product, (0, 0)))
        out_ref[...] = full_dot(product, inverse, (1, 1))
        return carry

    lax.fori_loop(0, ITERS, step, 0)


def iterate(pieces, places, start, total):
    width_x, rank = start.shape
    return pl.pallas_call(
        functools.partial(iterate_body, total),
        in_specs=[pl.BlockSpec(memory_space=pltpu.SMEM)]
        + [pl.BlockSpec(memory_space=pltpu.VMEM)] * (len(pieces) + 1),
        out_specs=pl.BlockSpec(memory_space=pltpu.VMEM),
        out_shape=jax.ShapeDtypeStruct((width_x, rank), F32),
        scratch_shapes=[pltpu.VMEM((width_x, width_x), F32)],
        compiler_params=pltpu.CompilerParams(vmem_limit_bytes=24 * MIB),
        cost_estimate=pl.CostEstimate(
            flops=4 * 10**10, bytes_accessed=8 * start.size, transcendentals=0
        ),
        name="subspace",
    )(places, *pieces, start)


def stack_body(places_ref, *refs):
    *piece_refs, out_ref = refs
    for i, piece_ref in enumerate(piece_refs):
        out_ref[places_ref[i]] = piece_ref[...]


def stack(pieces, places):
    return pl.pallas_call(
        stack_body,
        in_specs=[pl.BlockSpec(memory_space=pltpu.SMEM)]
        + [pl.BlockSpec(memory_space=pltpu.VMEM)] * len(pieces),
        out_specs=pl.BlockSpec(memory_space=pltpu.VMEM),
        out_shape=jax.ShapeDtypeStruct((len(pieces),) + pieces[0].shape, F32),
        compiler_params=pltpu.CompilerParams(vmem_limit_bytes=16 * MIB),
        name="stack_rows",
    )(places, *pieces)


def pack_body(first_ref, field_ref, out_ref):
    for z in range(field_ref.shape[1]):
        out_ref[z] = field_ref[:, z, :]


def pack(field, first, depth):
    x_block, _, y_block = field.shape
    return pl.pallas_call(
        pack_body,
        grid_spec=pltpu.PrefetchScalarGridSpec(
            num_scalar_prefetch=1,
            grid=(depth // TALL,),
            in_specs=[pl.BlockSpec((x_block, TALL, y_block), lambda i, at: (0, at[0] + i, 0))],
            out_specs=pl.BlockSpec((TALL, x_block, y_block), lambda i, at: (i, 0, 0)),
        ),
        out_shape=jax.ShapeDtypeStruct((depth, x_block, y_block), F32),
        compiler_params=pltpu.CompilerParams(vmem_limit_bytes=48 * MIB),
        cost_estimate=pl.CostEstimate(
            flops=0, bytes_accessed=8 * depth * x_block * y_block, transcendentals=0
        ),
        name="pack_z",
    )(first.astype(jnp.int32).reshape(1), field)


def tie(value, others):
    return lax.optimization_barrier((value, *others))[0] if others else value


class Line:
    def __init__(self):
        self.ends = []

    def done(self):
        last = len(self.ends) - WINDOW + 1
        return self.ends[max(0, last - 1) : max(0, last)]

    def send(self, cut, source, axis, perm):
        got = lax.ppermute(cut(tie(source, self.done())), axis, perm)
        self.ends.append(got)
        return got


def chunk_depths(groups):
    if groups < 4:
        return [groups]
    last = max(1, groups // 8)
    left = groups - 2 * last
    first = [(left + k) // 3 for k in (2, 1, 0)]
    return [depth for depth in first if depth] + [last, last]


def on_device(field, start):
    n = lax.axis_size("gx")
    m = lax.axis_size("yz")
    g = lax.axis_index("gx")
    q = lax.axis_index("yz")
    x_block, depth, y_block = field.shape
    width_x, width_y = x_block * n, y_block * m
    rank = start.shape[1]
    slab = depth // n
    line = LINE if n % LINE == 0 else 1
    rest = n // line
    order = Line()

    def moved(index, a, b, sign=1):
        return (index // rest + sign * a) % line * rest + (index % rest + sign * b) % rest

    def gx_perm(a, b):
        return [(i, moved(i, a, b)) for i in range(n)]

    def yz_perm(d):
        return [(i, (i + d) % m) for i in range(m)]

    far = sorted(range(1, line), key=lambda a: abs(2 * a - line))
    shifts = [(a, (b + k) % rest) for b in range(rest) for k, a in enumerate(far)]
    shifts[4:4] = [(0, b) for b in range(1, rest)]
    turns = sorted(range(1, m), key=lambda d: abs(2 * d - m))

    cells = jnp.zeros((slab // m, m, width_x, y_block), F32)

    def to_gx(first, zc, a, b, whole):
        place = (moved(g, a, b) * slab + first) // TALL
        got = order.send(lambda at: pack(field, at, zc), place, "gx", gx_perm(a, b))
        return lax.dynamic_update_slice_in_dim(whole, got[:, None], moved(g, a, b, -1), axis=1)

    def to_yz(cells, first, d, whole, after=()):
        zs = whole.shape[0] // m

        def cut(source):
            return lax.dynamic_slice_in_dim(source, (q + d) % m * zs, zs, axis=0)

        got = order.send(cut, tie(whole, after), "yz", yz_perm(d))
        return lax.dynamic_update_slice(cells, got[:, None], (first // m, (q - d) % m, 0, 0))

    gram = jnp.zeros((width_x, width_x), F32)
    before, start_z, first = None, 0, 0
    group = math.lcm(m, TALL)
    for groups in chunk_depths(slab // group):
        zc = groups * group
        units = zc // m
        whole = jnp.zeros((zc, n, x_block, y_block), F32)
        waiting = list(turns) if before is not None else []
        for k, (a, b) in enumerate(shifts):
            whole = to_gx(first, zc, a, b, whole)
            if k >= WINDOW - 1 and waiting:
                cells = to_yz(cells, start_z, waiting.pop(0), before)
        for d in waiting:
            cells = to_yz(cells, start_z, d, before)
        across = order.ends[-len(shifts) - len(turns) :]
        own = pack(field, (g * slab + first) // TALL, zc)[:, None]
        whole = lax.dynamic_update_slice_in_dim(whole, own, g, axis=1)
        before = whole.reshape(zc, width_x, y_block)
        gram = gram_of(before, gram)
        own = lax.dynamic_slice_in_dim(before, q * units, units, axis=0)
        cells = lax.dynamic_update_slice(cells, own[:, None], (first // m, q, 0, 0))
        start_z, first = first, first + zc

    rows = width_x // m
    slabs = tie(gram, across).reshape(m, rows, width_x)

    def pick(array, index):
        return lax.dynamic_index_in_dim(array, index, axis=0, keepdims=False)

    summed = pick(slabs, q)
    for d in turns:
        summed = summed + lax.ppermute(pick(slabs, (q + d) % m), "yz", yz_perm(d))
    cells = to_yz(cells, start_z, turns[0], before, [summed])
    strips = summed.reshape(n, rows // n, width_x)
    summed = pick(strips, g)
    for a, b in shifts:
        summed = summed + lax.ppermute(pick(strips, moved(g, a, b)), "gx", gx_perm(a, b))
    pieces = [summed] + [lax.ppermute(summed, "gx", gx_perm(a, b)) for a, b in shifts]
    places = jnp.stack([g] + [moved(g, a, b, -1) for a, b in shifts]).astype(jnp.int32)
    summed = stack(pieces, places).reshape(rows, width_x)
    pieces = [summed] + [lax.ppermute(summed, "yz", yz_perm(d)) for d in turns]
    places = jnp.stack([q] + [(q - d) % m for d in turns]).astype(jnp.int32)
    for d in turns[1:]:
        cells = to_yz(cells, start_z, d, before, pieces[1:])
    basis = iterate(pieces, places, start, float(width_y * depth))

    partial_y = core_gram(cells, basis, float(rank * depth))
    cores = 2 if m % 2 == 0 else 1
    chips = m // cores
    core, chip = q % cores, q // cores
    blocks = partial_y.reshape(chips, cores, y_block, width_y)

    def of_core(index):
        return lax.dynamic_index_in_dim(blocks, index, axis=1, keepdims=False)

    blocks_here = of_core(core)
    for d in range(1, cores):
        perm = [(i, i // cores * cores + (i + d) % cores) for i in range(m)]
        blocks_here = blocks_here + lax.ppermute(of_core((core + d) % cores), "yz", perm)
    rows_y = pick(blocks_here, chip)
    for d in range(1, chips):
        perm = [(i, (i + d * cores) % m) for i in range(m)]
        rows_y = rows_y + lax.ppermute(pick(blocks_here, (chip + d) % chips), "yz", perm)
    width = width_y // n

    def block(index):
        return lax.dynamic_slice_in_dim(rows_y, index * width, width, axis=1)

    gram_y = block(g)
    for a, b in shifts:
        gram_y = gram_y + lax.ppermute(block(moved(g, a, b)), "gx", gx_perm(a, b))
    return (basis, gram_y)


def solution(mesh):
    placed = (P("gx", None, "yz"), P())
    return jax.shard_map(
        on_device, mesh=mesh, in_specs=placed, out_specs=(P(), P("yz", "gx")), check_vma=False
    )
```

```python
import functools
import math

import jax
import jax.numpy as jnp
from jax import lax
from jax.experimental import pallas as pl
from jax.experimental.pallas import tpu as pltpu
from jax.sharding import PartitionSpec as P

ITERS = 4
WINDOW = 5
AHEAD = 2
TALL = 8
LINE = 4
MIB = 1024 * 1024
F32 = jnp.float32
BF16 = jnp.bfloat16


def halves(value):
    high = value.astype(BF16)
    low = (value - high.astype(F32)).astype(BF16)
    return high, low


def dot_nt(left, right):
    return lax.dot_general(left, right, (((1,), (1,)), ((), ())), preferred_element_type=F32)


def dot_tn(left, right):
    return lax.dot_general(left, right, (((0,), (0,)), ((), ())), preferred_element_type=F32)


def gram_body(steps, slab_ref, before_ref, out_ref, main, cross):
    step = pl.program_id(0)

    @pl.when(step == 0)
    def _():
        main[...] = jnp.zeros_like(main)
        cross[...] = jnp.zeros_like(cross)

    depth = slab_ref.shape[0]
    parts = [halves(slab_ref[z]) for z in range(depth)]
    high = jnp.concatenate([part[0] for part in parts], axis=1)
    low = jnp.concatenate([part[1] for part in parts], axis=1)
    main[...] += dot_nt(high, high)
    cross[...] += dot_nt(high, low)

    @pl.when(step == steps - 1)
    def _():
        mixed = cross[...]
        out_ref[...] = before_ref[...] + main[...] + mixed + mixed.T


def gram_of(slab, before):
    depth, width_x, width_y = slab.shape
    block = 4 if depth % 4 == 0 else 1
    steps = depth // block
    square = pl.BlockSpec((width_x, width_x), lambda i: (0, 0))
    return pl.pallas_call(
        functools.partial(gram_body, steps),
        grid=(steps,),
        in_specs=[pl.BlockSpec((block, width_x, width_y), lambda i: (i, 0, 0)), square],
        out_specs=square,
        out_shape=jax.ShapeDtypeStruct((width_x, width_x), F32),
        scratch_shapes=[pltpu.VMEM((width_x, width_x), F32)] * 2,
        compiler_params=pltpu.CompilerParams(vmem_limit_bytes=32 * MIB),
        cost_estimate=pl.CostEstimate(
            flops=4 * width_x * width_x * depth * width_y,
            bytes_accessed=slab.size * 4,
            transcendentals=0,
        ),
        name="gram_x",
    )(slab, before)


def core_body(steps, total, field_ref, basis_ref, out_ref, stacked_ref, high_ref, low_ref, main, cross):
    step = pl.program_id(0)
    rank = basis_ref.shape[1]

    @pl.when(step == 0)
    def _():
        main[...] = jnp.zeros_like(main)
        cross[...] = jnp.zeros_like(cross)
        basis_high, basis_low = halves(basis_ref[...].T)
        stacked_ref[:rank] = basis_high
        stacked_ref[rank:] = basis_low

    depth, blocks, _, width = field_ref.shape
    stacked = stacked_ref[...]
    for z in range(depth):
        for b in range(blocks):
            high, low = halves(field_ref[z, b])
            both = jnp.dot(stacked, high, preferred_element_type=F32)
            core = both[:rank] + both[rank:]
            core += jnp.dot(stacked[:rank], low, preferred_element_type=F32)
            core_high, core_low = halves(core)
            high_ref[pl.ds(z * rank, rank), pl.ds(b * width, width)] = core_high
            low_ref[pl.ds(z * rank, rank), pl.ds(b * width, width)] = core_low
    high = high_ref[...]
    main[...] += dot_tn(high, high)
    cross[...] += dot_tn(high, low_ref[...])

    @pl.when(step == steps - 1)
    def _():
        mixed = cross[...]
        out_ref[...] = (main[...] + mixed + mixed.T) / total


def core_gram(cells, basis, total):
    depth, blocks, width_x, width = cells.shape
    rank = basis.shape[1]
    width_y = blocks * width
    block = 2 if depth % 2 == 0 else 1
    steps = depth // block
    return pl.pallas_call(
        functools.partial(core_body, steps, total),
        grid=(steps,),
        in_specs=[
            pl.BlockSpec((block, blocks, width_x, width), lambda i: (i, 0, 0, 0)),
            pl.BlockSpec((width_x, rank), lambda i: (0, 0)),
        ],
        out_specs=pl.BlockSpec((width_y, width_y), lambda i: (0, 0)),
        out_shape=jax.ShapeDtypeStruct((width_y, width_y), F32),
        scratch_shapes=[
            pltpu.VMEM((2 * rank, width_x), BF16),
            pltpu.VMEM((block * rank, width_y), BF16),
            pltpu.VMEM((block * rank, width_y), BF16),
            pltpu.VMEM((width_y, width_y), F32),
            pltpu.VMEM((width_y, width_y), F32),
        ],
        compiler_params=pltpu.CompilerParams(vmem_limit_bytes=48 * MIB),
        cost_estimate=pl.CostEstimate(
            flops=6 * rank * cells.size + 4 * rank * depth * width_y * width_y,
            bytes_accessed=cells.size * 4,
            transcendentals=0,
        ),
        name="core_gram_y",
    )(cells, basis)


def full_dot(left, right, contract):
    return lax.dot_general(
        left,
        right,
        ((contract[:1], contract[1:]), ((), ())),
        precision=lax.Precision.HIGHEST,
        preferred_element_type=F32,
    )


def inverse_factor(cross):
    size = cross.shape[0]
    tall = 8
    wide = 4
    groups = size // tall
    shape = (tall, size)
    sublane = lax.broadcasted_iota(jnp.int32, shape, 0)
    lane = lax.broadcasted_iota(jnp.int32, shape, 1)
    left = [cross[t * tall : (t + 1) * tall] for t in range(groups)]
    right = [(lane == sublane + t * tall).astype(F32) for t in range(groups)]
    pivots = [jnp.ones(shape, F32) for _ in range(groups)]

    def row(value, s):
        return jnp.broadcast_to(value[s : s + 1, :], shape)

    for first in range(0, size, wide):
        top, s0 = first // tall, first % tall
        below = range(top, groups)
        columns = [
            {t: jnp.broadcast_to(left[t][:, first + k : first + k + 1], shape) for t in below}
            for k in range(wide)
        ]
        rows = [row(left[top], s0 + k) for k in range(wide)]
        eyes = [row(right[top], s0 + k) for k in range(wide)]
        scaled = []
        for i in range(wide):
            pivot = row(columns[i][top], s0 + i)
            inverse = 1.0 / pivot
            scaled.append((rows[i] * inverse, eyes[i] * inverse))
            for k in range(i + 1, wide):
                ratio = row(columns[i][top], s0 + k) * inverse
                for t in below:
                    columns[k][t] = columns[k][t] - ratio * columns[i][t]
                rows[k] = rows[k] - ratio * rows[i]
                eyes[k] = eyes[k] - ratio * eyes[i]
            here = sublane == s0 + i
            pivots[top] = jnp.where(here, pivot, pivots[top])
        rest = sublane >= s0 + wide
        for t in below:
            new_left, new_right = left[t], right[t]
            for i in range(wide):
                new_left = new_left - columns[i][t] * scaled[i][0]
                new_right = new_right - columns[i][t] * scaled[i][1]
            if t == top:
                new_left = jnp.where(rest, new_left, left[t])
                new_right = jnp.where(rest, new_right, right[t])
                for i in range(wide):
                    new_right = jnp.where(sublane == s0 + i, eyes[i], new_right)
            left[t], right[t] = new_left, new_right
    for t in range(groups):
        root = lax.rsqrt(pivots[t])
        root = root * (1.5 - 0.5 * pivots[t] * root * root)
        right[t] = right[t] * root
    return jnp.concatenate(right, axis=0)


def iterate_body(total, places_ref, *refs):
    *piece_refs, start_ref, out_ref, gram = refs
    height = piece_refs[0].shape[0]
    for i, piece_ref in enumerate(piece_refs):
        place = pl.multiple_of(places_ref[i] * height, height)
        gram[pl.ds(place, height)] = piece_ref[...] / total
    out_ref[...] = start_ref[...]

    def step(_, carry):
        product = full_dot(gram[...], out_ref[...], (1, 0))
        inverse = inverse_factor(full_dot(product, product, (0, 0)))
        out_ref[...] = full_dot(product, inverse, (1, 1))
        return carry

    lax.fori_loop(0, ITERS, step, 0)


def iterate(pieces, places, start, total):
    width_x, rank = start.shape
    return pl.pallas_call(
        functools.partial(iterate_body, total),
        in_specs=[pl.BlockSpec(memory_space=pltpu.SMEM)]
        + [pl.BlockSpec(memory_space=pltpu.VMEM)] * (len(pieces) + 1),
        out_specs=pl.BlockSpec(memory_space=pltpu.VMEM),
        out_shape=jax.ShapeDtypeStruct((width_x, rank), F32),
        scratch_shapes=[pltpu.VMEM((width_x, width_x), F32)],
        compiler_params=pltpu.CompilerParams(vmem_limit_bytes=24 * MIB),
        cost_estimate=pl.CostEstimate(
            flops=4 * 10**10, bytes_accessed=8 * start.size, transcendentals=0
        ),
        name="subspace",
    )(places, *pieces, start)


def stack_body(places_ref, *refs):
    *piece_refs, out_ref = refs
    for i, piece_ref in enumerate(piece_refs):
        out_ref[places_ref[i]] = piece_ref[...]


def stack(pieces, places):
    return pl.pallas_call(
        stack_body,
        in_specs=[pl.BlockSpec(memory_space=pltpu.SMEM)]
        + [pl.BlockSpec(memory_space=pltpu.VMEM)] * len(pieces),
        out_specs=pl.BlockSpec(memory_space=pltpu.VMEM),
        out_shape=jax.ShapeDtypeStruct((len(pieces),) + pieces[0].shape, F32),
        compiler_params=pltpu.CompilerParams(vmem_limit_bytes=16 * MIB),
        name="stack_rows",
    )(places, *pieces)


def pack_body(first_ref, field_ref, out_ref):
    for z in range(field_ref.shape[1]):
        out_ref[z] = field_ref[:, z, :]


def pack(field, first, depth):
    x_block, _, y_block = field.shape
    return pl.pallas_call(
        pack_body,
        grid_spec=pltpu.PrefetchScalarGridSpec(
            num_scalar_prefetch=1,
            grid=(depth // TALL,),
            in_specs=[pl.BlockSpec((x_block, TALL, y_block), lambda i, at: (0, at[0] + i, 0))],
            out_specs=pl.BlockSpec((TALL, x_block, y_block), lambda i, at: (i, 0, 0)),
        ),
        out_shape=jax.ShapeDtypeStruct((depth, x_block, y_block), F32),
        compiler_params=pltpu.CompilerParams(vmem_limit_bytes=48 * MIB),
        cost_estimate=pl.CostEstimate(
            flops=0, bytes_accessed=8 * depth * x_block * y_block, transcendentals=0
        ),
        name="pack_z",
    )(first.astype(jnp.int32).reshape(1), field)


def tie(value, others):
    return lax.optimization_barrier((value, *others))[0] if others else value


class Line:
    def __init__(self):
        self.ends = []

    def done(self, ahead):
        last = len(self.ends) - WINDOW + 1 - ahead
        return self.ends[max(0, last - 1) : max(0, last)]

    def send(self, cut, source, axis, perm):
        value = cut(tie(source, self.done(AHEAD)))
        got = lax.ppermute(tie(value, self.done(0)), axis, perm)
        self.ends.append(got)
        return got


def chunk_depths(groups):
    if groups < 4:
        return [groups]
    last = max(1, groups // 8)
    left = groups - 2 * last
    first = [(left + k) // 3 for k in (2, 1, 0)]
    return [depth for depth in first if depth] + [last, last]


def on_device(field, start):
    n = lax.axis_size("gx")
    m = lax.axis_size("yz")
    g = lax.axis_index("gx")
    q = lax.axis_index("yz")
    x_block, depth, y_block = field.shape
    width_x, width_y = x_block * n, y_block * m
    rank = start.shape[1]
    slab = depth // n
    line = LINE if n % LINE == 0 else 1
    rest = n // line
    order = Line()

    def moved(index, a, b, sign=1):
        return (index // rest + sign * a) % line * rest + (index % rest + sign * b) % rest

    def gx_perm(a, b):
        return [(i, moved(i, a, b)) for i in range(n)]

    def yz_perm(d):
        return [(i, (i + d) % m) for i in range(m)]

    far = sorted(range(1, line), key=lambda a: abs(2 * a - line))
    shifts = [(a, (b + k) % rest) for b in range(rest) for k, a in enumerate(far)]
    shifts[4:4] = [(0, b) for b in range(1, rest)]
    turns = sorted(range(1, m), key=lambda d: abs(2 * d - m))

    cells = jnp.zeros((slab // m, m, width_x, y_block), F32)

    def to_gx(first, zc, a, b, whole):
        place = (moved(g, a, b) * slab + first) // TALL
        got = order.send(lambda at: pack(field, at, zc), place, "gx", gx_perm(a, b))
        return lax.dynamic_update_slice_in_dim(whole, got[:, None], moved(g, a, b, -1), axis=1)

    def to_yz(cells, first, d, whole, after=()):
        zs = whole.shape[0] // m

        def cut(source):
            return lax.dynamic_slice_in_dim(source, (q + d) % m * zs, zs, axis=0)

        got = order.send(cut, tie(whole, after), "yz", yz_perm(d))
        return lax.dynamic_update_slice(cells, got[:, None], (first // m, (q - d) % m, 0, 0))

    gram = jnp.zeros((width_x, width_x), F32)
    before, start_z, first = None, 0, 0
    group = math.lcm(m, TALL)
    for groups in chunk_depths(slab // group):
        zc = groups * group
        units = zc // m
        whole = jnp.zeros((zc, n, x_block, y_block), F32)
        waiting = list(turns) if before is not None else []
        for k, (a, b) in enumerate(shifts):
            whole = to_gx(first, zc, a, b, whole)
            if k >= WINDOW - 1 and waiting:
                cells = to_yz(cells, start_z, waiting.pop(0), before)
        for d in waiting:
            cells = to_yz(cells, start_z, d, before)
        across = order.ends[-len(shifts) - len(turns) :]
        own = pack(field, (g * slab + first) // TALL, zc)[:, None]
        whole = lax.dynamic_update_slice_in_dim(whole, own, g, axis=1)
        before = whole.reshape(zc, width_x, y_block)
        gram = gram_of(before, gram)
        own = lax.dynamic_slice_in_dim(before, q * units, units, axis=0)
        cells = lax.dynamic_update_slice(cells, own[:, None], (first // m, q, 0, 0))
        start_z, first = first, first + zc

    rows = width_x // m
    slabs = tie(gram, across).reshape(m, rows, width_x)

    def pick(array, index):
        return lax.dynamic_index_in_dim(array, index, axis=0, keepdims=False)

    summed = pick(slabs, q)
    for d in turns:
        summed = summed + lax.ppermute(pick(slabs, (q + d) % m), "yz", yz_perm(d))
    cells = to_yz(cells, start_z, turns[0], before, [summed])
    strips = summed.reshape(n, rows // n, width_x)
    summed = pick(strips, g)
    for a, b in shifts:
        summed = summed + lax.ppermute(pick(strips, moved(g, a, b)), "gx", gx_perm(a, b))
    pieces = [summed] + [lax.ppermute(summed, "gx", gx_perm(a, b)) for a, b in shifts]
    places = jnp.stack([g] + [moved(g, a, b, -1) for a, b in shifts]).astype(jnp.int32)
    summed = stack(pieces, places).reshape(rows, width_x)
    pieces = [summed] + [lax.ppermute(summed, "yz", yz_perm(d)) for d in turns]
    places = jnp.stack([q] + [(q - d) % m for d in turns]).astype(jnp.int32)
    for d in turns[1:]:
        cells = to_yz(cells, start_z, d, before, pieces[1:])
    basis = iterate(pieces, places, start, float(width_y * depth))

    partial_y = core_gram(cells, basis, float(rank * depth))
    cores = 2 if m % 2 == 0 else 1
    chips = m // cores
    core, chip = q % cores, q // cores
    blocks = partial_y.reshape(chips, cores, y_block, width_y)

    def of_core(index):
        return lax.dynamic_index_in_dim(blocks, index, axis=1, keepdims=False)

    blocks_here = of_core(core)
    for d in range(1, cores):
        perm = [(i, i // cores * cores + (i + d) % cores) for i in range(m)]
        blocks_here = blocks_here + lax.ppermute(of_core((core + d) % cores), "yz", perm)
    rows_y = pick(blocks_here, chip)
    for d in range(1, chips):
        perm = [(i, (i + d * cores) % m) for i in range(m)]
        rows_y = rows_y + lax.ppermute(pick(blocks_here, (chip + d) % chips), "yz", perm)
    width = width_y // n

    def block(index):
        return lax.dynamic_slice_in_dim(rows_y, index * width, width, axis=1)

    gram_y = block(g)
    for a, b in shifts:
        gram_y = gram_y + lax.ppermute(block(moved(g, a, b)), "gx", gx_perm(a, b))
    return (basis, gram_y)


def solution(mesh):
    placed = (P("gx", None, "yz"), P())
    return jax.shard_map(
        on_device, mesh=mesh, in_specs=placed, out_specs=(P(), P("yz", "gx")), check_vma=False
    )
```

```python
import functools
import math

import jax
import jax.numpy as jnp
from jax import lax
from jax.experimental import pallas as pl
from jax.experimental.pallas import tpu as pltpu
from jax.sharding import PartitionSpec as P

ITERS = 4
WINDOW = 14
AHEAD = 2
CORE = -2
CHIP = -5
TALL = 8
LINE = 4
MIB = 1024 * 1024
F32 = jnp.float32
BF16 = jnp.bfloat16


def halves(value):
    high = value.astype(BF16)
    low = (value - high.astype(F32)).astype(BF16)
    return high, low


def dot_nt(left, right):
    return lax.dot_general(left, right, (((1,), (1,)), ((), ())), preferred_element_type=F32)


def dot_tn(left, right):
    return lax.dot_general(left, right, (((0,), (0,)), ((), ())), preferred_element_type=F32)


def gram_body(steps, slab_ref, before_ref, out_ref, main, cross):
    step = pl.program_id(0)

    @pl.when(step == 0)
    def _():
        main[...] = jnp.zeros_like(main)
        cross[...] = jnp.zeros_like(cross)

    depth = slab_ref.shape[0]
    parts = [halves(slab_ref[z]) for z in range(depth)]
    high = jnp.concatenate([part[0] for part in parts], axis=1)
    low = jnp.concatenate([part[1] for part in parts], axis=1)
    main[...] += dot_nt(high, high)
    cross[...] += dot_nt(high, low)

    @pl.when(step == steps - 1)
    def _():
        mixed = cross[...]
        out_ref[...] = before_ref[...] + main[...] + mixed + mixed.T


def gram_of(slab, before):
    depth, width_x, width_y = slab.shape
    block = 4 if depth % 4 == 0 else 1
    steps = depth // block
    square = pl.BlockSpec((width_x, width_x), lambda i: (0, 0))
    return pl.pallas_call(
        functools.partial(gram_body, steps),
        grid=(steps,),
        in_specs=[pl.BlockSpec((block, width_x, width_y), lambda i: (i, 0, 0)), square],
        out_specs=square,
        out_shape=jax.ShapeDtypeStruct((width_x, width_x), F32),
        scratch_shapes=[pltpu.VMEM((width_x, width_x), F32)] * 2,
        compiler_params=pltpu.CompilerParams(vmem_limit_bytes=32 * MIB),
        cost_estimate=pl.CostEstimate(
            flops=4 * width_x * width_x * depth * width_y,
            bytes_accessed=slab.size * 4,
            transcendentals=0,
        ),
        name="gram_x",
    )(slab, before)


def core_body(steps, total, field_ref, basis_ref, out_ref, stacked_ref, high_ref, low_ref, main, cross):
    step = pl.program_id(0)
    rank = basis_ref.shape[1]

    @pl.when(step == 0)
    def _():
        main[...] = jnp.zeros_like(main)
        cross[...] = jnp.zeros_like(cross)
        basis_high, basis_low = halves(basis_ref[...].T)
        stacked_ref[:rank] = basis_high
        stacked_ref[rank:] = basis_low

    depth, blocks, _, width = field_ref.shape
    stacked = stacked_ref[...]
    for z in range(depth):
        for b in range(blocks):
            high, low = halves(field_ref[z, b])
            both = jnp.dot(stacked, high, preferred_element_type=F32)
            core = both[:rank] + both[rank:]
            core += jnp.dot(stacked[:rank], low, preferred_element_type=F32)
            core_high, core_low = halves(core)
            high_ref[pl.ds(z * rank, rank), pl.ds(b * width, width)] = core_high
            low_ref[pl.ds(z * rank, rank), pl.ds(b * width, width)] = core_low
    high = high_ref[...]
    main[...] += dot_tn(high, high)
    cross[...] += dot_tn(high, low_ref[...])

    @pl.when(step == steps - 1)
    def _():
        mixed = cross[...]
        out_ref[...] = (main[...] + mixed + mixed.T) / total


def core_gram(cells, basis, total):
    depth, blocks, width_x, width = cells.shape
    rank = basis.shape[1]
    width_y = blocks * width
    block = 2 if depth % 2 == 0 else 1
    steps = depth // block
    return pl.pallas_call(
        functools.partial(core_body, steps, total),
        grid=(steps,),
        in_specs=[
            pl.BlockSpec((block, blocks, width_x, width), lambda i: (i, 0, 0, 0)),
            pl.BlockSpec((width_x, rank), lambda i: (0, 0)),
        ],
        out_specs=pl.BlockSpec((width_y, width_y), lambda i: (0, 0)),
        out_shape=jax.ShapeDtypeStruct((width_y, width_y), F32),
        scratch_shapes=[
            pltpu.VMEM((2 * rank, width_x), BF16),
            pltpu.VMEM((block * rank, width_y), BF16),
            pltpu.VMEM((block * rank, width_y), BF16),
            pltpu.VMEM((width_y, width_y), F32),
            pltpu.VMEM((width_y, width_y), F32),
        ],
        compiler_params=pltpu.CompilerParams(vmem_limit_bytes=48 * MIB),
        cost_estimate=pl.CostEstimate(
            flops=6 * rank * cells.size + 4 * rank * depth * width_y * width_y,
            bytes_accessed=cells.size * 4,
            transcendentals=0,
        ),
        name="core_gram_y",
    )(cells, basis)


def full_dot(left, right, contract):
    return lax.dot_general(
        left,
        right,
        ((contract[:1], contract[1:]), ((), ())),
        precision=lax.Precision.HIGHEST,
        preferred_element_type=F32,
    )


def inverse_factor(cross):
    size = cross.shape[0]
    wide = 4
    groups = size // TALL
    shape = (TALL, size)
    sublane = lax.broadcasted_iota(jnp.int32, shape, 0)
    lane = lax.broadcasted_iota(jnp.int32, shape, 1)
    left = [cross[t * TALL : (t + 1) * TALL] for t in range(groups)]
    right = [(lane == sublane + t * TALL).astype(F32) for t in range(groups)]
    pivots = [jnp.ones(shape, F32) for _ in range(groups)]
    ratios = [jnp.zeros(shape, F32) for _ in range(groups)]

    def row(value, s):
        return jnp.broadcast_to(value[s : s + 1, :], shape)

    for first in range(0, size, wide):
        top, s0 = first // TALL, first % TALL
        below = range(top, groups)
        columns = [
            {t: jnp.broadcast_to(left[t][:, first + k : first + k + 1], shape) for t in below}
            for k in range(wide)
        ]
        rows = [row(left[top], s0 + k) for k in range(wide)]
        eyes = [row(right[top], s0 + k) for k in range(wide)]
        for i in range(0, wide, 2):
            a = row(columns[i][top], s0 + i)
            b = row(columns[i][top], s0 + i + 1)
            c = row(columns[i + 1][top], s0 + i + 1)
            inverse = 1.0 / (a * c - b * b)
            solved = (
                (rows[i] * c - rows[i + 1] * b) * inverse,
                (rows[i + 1] * a - rows[i] * b) * inverse,
                (eyes[i] * c - eyes[i + 1] * b) * inverse,
                (eyes[i + 1] * a - eyes[i] * b) * inverse,
            )
            ratio = b / a
            pivots[top] = jnp.where(sublane == s0 + i, a, pivots[top])
            pivots[top] = jnp.where(sublane == s0 + i + 1, c - b * ratio, pivots[top])
            ratios[top] = jnp.where(sublane == s0 + i + 1, ratio, ratios[top])
            for k in range(i + 2, wide):
                one, two = (row(columns[j][top], s0 + k) for j in (i, i + 1))
                first_part = (one * c - two * b) * inverse
                second_part = (two * a - one * b) * inverse
                for t in below:
                    columns[k][t] = columns[k][t] - (
                        first_part * columns[i][t] + second_part * columns[i + 1][t]
                    )
                rows[k] = rows[k] - (first_part * rows[i] + second_part * rows[i + 1])
                eyes[k] = eyes[k] - (first_part * eyes[i] + second_part * eyes[i + 1])
            rest = sublane >= s0 + wide
            for t in below:
                one, two = columns[i][t], columns[i + 1][t]
                new_left = left[t] - (one * solved[0] + two * solved[1])
                new_right = right[t] - (one * solved[2] + two * solved[3])
                if t == top:
                    new_left = jnp.where(rest, new_left, left[t])
                    new_right = jnp.where(rest, new_right, right[t])
                    for j in (i, i + 1):
                        new_right = jnp.where(sublane == s0 + j, eyes[j], new_right)
                left[t], right[t] = new_left, new_right
    for t in range(groups):
        above = jnp.concatenate([right[t][:1], right[t][:-1]], axis=0)
        value = right[t] - ratios[t] * above
        root = lax.rsqrt(pivots[t])
        root = root * (1.5 - 0.5 * pivots[t] * root * root)
        right[t] = value * root
    return jnp.concatenate(right, axis=0)


def iterate_body(total, places_ref, *refs):
    *piece_refs, start_ref, out_ref, gram = refs
    height = piece_refs[0].shape[0]
    for i, piece_ref in enumerate(piece_refs):
        place = pl.multiple_of(places_ref[i] * height, height)
        gram[pl.ds(place, height)] = piece_ref[...] / total
    out_ref[...] = start_ref[...]

    def step(_, carry):
        product = full_dot(gram[...], out_ref[...], (1, 0))
        product = product * lax.rsqrt(jnp.sum(product * product, axis=0, keepdims=True))
        inverse = inverse_factor(full_dot(product, product, (0, 0)))
        out_ref[...] = full_dot(product, inverse, (1, 1))
        return carry

    lax.fori_loop(0, ITERS, step, 0)


def iterate(pieces, places, start, total):
    width_x, rank = start.shape
    return pl.pallas_call(
        functools.partial(iterate_body, total),
        in_specs=[pl.BlockSpec(memory_space=pltpu.SMEM)]
        + [pl.BlockSpec(memory_space=pltpu.VMEM)] * (len(pieces) + 1),
        out_specs=pl.BlockSpec(memory_space=pltpu.VMEM),
        out_shape=jax.ShapeDtypeStruct((width_x, rank), F32),
        scratch_shapes=[pltpu.VMEM((width_x, width_x), F32)],
        compiler_params=pltpu.CompilerParams(vmem_limit_bytes=24 * MIB),
        cost_estimate=pl.CostEstimate(
            flops=4 * 10**10, bytes_accessed=8 * start.size, transcendentals=0
        ),
        name="subspace",
    )(places, *pieces, start)


def stack_body(places_ref, *refs):
    *piece_refs, out_ref = refs
    for i, piece_ref in enumerate(piece_refs):
        out_ref[places_ref[i]] = piece_ref[...]


def stack(pieces, places):
    return pl.pallas_call(
        stack_body,
        in_specs=[pl.BlockSpec(memory_space=pltpu.SMEM)]
        + [pl.BlockSpec(memory_space=pltpu.VMEM)] * len(pieces),
        out_specs=pl.BlockSpec(memory_space=pltpu.VMEM),
        out_shape=jax.ShapeDtypeStruct((len(pieces),) + pieces[0].shape, F32),
        compiler_params=pltpu.CompilerParams(vmem_limit_bytes=16 * MIB),
        name="stack_rows",
    )(places, *pieces)


def pack_body(first_ref, field_ref, out_ref):
    for z in range(field_ref.shape[1]):
        out_ref[z] = field_ref[:, z, :]


def pack(field, first, depth):
    x_block, _, y_block = field.shape
    return pl.pallas_call(
        pack_body,
        grid_spec=pltpu.PrefetchScalarGridSpec(
            num_scalar_prefetch=1,
            grid=(depth // TALL,),
            in_specs=[pl.BlockSpec((x_block, TALL, y_block), lambda i, at: (0, at[0] + i, 0))],
            out_specs=pl.BlockSpec((TALL, x_block, y_block), lambda i, at: (i, 0, 0)),
        ),
        out_shape=jax.ShapeDtypeStruct((depth, x_block, y_block), F32),
        compiler_params=pltpu.CompilerParams(vmem_limit_bytes=48 * MIB),
        cost_estimate=pl.CostEstimate(
            flops=0, bytes_accessed=1, transcendentals=0
        ),
        name="pack_z",
    )(first.astype(jnp.int32).reshape(1), field)


def tie(value, others):
    return lax.optimization_barrier((value, *others))[0] if others else value


class Line:
    def __init__(self):
        self.ends = []

    def done(self, ahead):
        last = len(self.ends) - WINDOW + 1 - ahead
        return self.ends[max(0, last - 1) : max(0, last)]

    def send(self, cut, index, axis, perm, after=()):
        value = cut(tie(index, self.done(AHEAD)))
        got = lax.ppermute(tie(value, self.done(0) + list(after)), axis, perm)
        self.ends.append(got)
        return got


def chunk_depths(groups):
    if groups < 4:
        return [groups]
    last = max(1, groups // 8)
    left = groups - 2 * last
    first = [(left + k) // 3 for k in (2, 1, 0)]
    return [depth for depth in first if depth] + [last, last]


def on_device(field, start):
    n = lax.axis_size("gx")
    m = lax.axis_size("yz")
    g = lax.axis_index("gx")
    q = lax.axis_index("yz")
    x_block, depth, y_block = field.shape
    width_x, width_y = x_block * n, y_block * m
    rank = start.shape[1]
    slab = depth // n
    line = LINE if n % LINE == 0 else 1
    rest = n // line
    order = Line()

    def moved(index, a, b, sign=1):
        return (index // rest + sign * a) % line * rest + (index % rest + sign * b) % rest

    def gx_perm(a, b):
        return [(i, moved(i, a, b)) for i in range(n)]

    def yz_perm(d):
        return [(i, (i + d) % m) for i in range(m)]

    far = sorted(range(1, line), key=lambda a: abs(2 * a - line))
    shifts = [(a, (b + k) % rest) for b in range(rest) for k, a in enumerate(far)]
    shifts[4:4] = [(0, b) for b in range(1, rest)]
    turns = sorted(range(1, m), key=lambda d: abs(2 * d - m))

    cells = jnp.zeros((slab // m, m, width_x, y_block), F32)

    def to_gx(first, zc, a, b, whole, after):
        place = (moved(g, a, b) * slab + first) // TALL
        got = order.send(lambda at: pack(field, at, zc), place, "gx", gx_perm(a, b), after)
        return lax.dynamic_update_slice_in_dim(whole, got[:, None], moved(g, a, b, -1), axis=1)

    cores = 2 if m % 2 == 0 else 1
    chips = m // cores
    core, chip = q % cores, q // cores

    def core_perm(d):
        return [(i, i // cores * cores + (i + d) % cores) for i in range(m)]

    def chip_perm(d):
        return [(i, (i + d * cores) % m) for i in range(m)]

    def part(array, index, count):
        depth = array.shape[0] // count
        return lax.dynamic_slice_in_dim(array, index * depth, depth, axis=0)

    def to_core(whole):
        both = jnp.zeros((whole.shape[0] // cores, cores, width_x, y_block), F32)
        own = part(whole, core, cores)[:, None]
        both = lax.dynamic_update_slice_in_dim(both, own, core, axis=1)
        for d in range(1, cores):
            cut = part(whole, (core + d) % cores, cores)
            got = lax.ppermute(cut, "yz", core_perm(d))
            both = lax.dynamic_update_slice_in_dim(both, got[:, None], (core - d) % cores, axis=1)
        return both

    def to_chip(cells, first, both, after=()):
        def put(cells, value, source):
            return lax.dynamic_update_slice(cells, value, (first // m, source * cores, 0, 0))

        cells, ends = put(cells, part(both, chip, chips), chip), []
        for d in range(1, chips):
            cut = part(tie(both, after), (chip + d) % chips, chips)
            got = lax.ppermute(cut, "yz", chip_perm(d))
            ends.append(got)
            cells = put(cells, got, (chip - d) % chips)
        return cells, ends

    gram = jnp.zeros((width_x, width_x), F32)
    before, start_z, first, across = None, 0, 0, []
    group = math.lcm(m, TALL)
    for groups in chunk_depths(slab // group):
        zc = groups * group
        whole = jnp.zeros((zc, n, x_block, y_block), F32)
        if before is not None:
            both = to_core(before)
            cells, ends = to_chip(cells, start_z, both)
            across.append(ends)
        for k, (a, b) in enumerate(shifts):
            after = []
            if k == len(shifts) + CORE and before is not None:
                after = [both]
            if k == len(shifts) + CHIP and len(across) > 1:
                after = across[-2]
            whole = to_gx(first, zc, a, b, whole, after)
        own = pack(field, (g * slab + first) // TALL, zc)[:, None]
        whole = lax.dynamic_update_slice_in_dim(whole, own, g, axis=1)
        before = whole.reshape(zc, width_x, y_block)
        gram = gram_of(before, gram)
        start_z, first = first, first + zc

    rows = width_x // m
    both = to_core(before)
    slabs = tie(gram, across[-1] if across else []).reshape(m, rows, width_x)

    def pick(array, index):
        return lax.dynamic_index_in_dim(array, index, axis=0, keepdims=False)

    summed = pick(slabs, q)
    for d in turns:
        summed = summed + lax.ppermute(pick(slabs, (q + d) % m), "yz", yz_perm(d))
    cells, _ = to_chip(cells, start_z, both, [summed])
    strips = summed.reshape(n, rows // n, width_x)
    summed = pick(strips, g)
    for a, b in shifts:
        summed = summed + lax.ppermute(pick(strips, moved(g, a, b)), "gx", gx_perm(a, b))
    pieces = [summed] + [lax.ppermute(summed, "gx", gx_perm(a, b)) for a, b in shifts]
    places = jnp.stack([g] + [moved(g, a, b, -1) for a, b in shifts]).astype(jnp.int32)
    summed = stack(pieces, places).reshape(rows, width_x)
    pieces = [summed] + [lax.ppermute(summed, "yz", yz_perm(d)) for d in turns]
    places = jnp.stack([q] + [(q - d) % m for d in turns]).astype(jnp.int32)
    basis = iterate(pieces, places, start, float(width_y * depth))

    partial_y = core_gram(cells, basis, float(rank * depth))
    blocks = partial_y.reshape(chips, cores, y_block, width_y)

    def of_core(index):
        return lax.dynamic_index_in_dim(blocks, index, axis=1, keepdims=False)

    blocks_here = of_core(core)
    for d in range(1, cores):
        blocks_here = blocks_here + lax.ppermute(
            of_core((core + d) % cores), "yz", core_perm(d)
        )
    rows_y = pick(blocks_here, chip)
    for d in range(1, chips):
        rows_y = rows_y + lax.ppermute(
            pick(blocks_here, (chip + d) % chips), "yz", chip_perm(d)
        )
    width = width_y // n

    def block(index):
        return lax.dynamic_slice_in_dim(rows_y, index * width, width, axis=1)

    gram_y = block(g)
    for a, b in shifts:
        gram_y = gram_y + lax.ppermute(block(moved(g, a, b)), "gx", gx_perm(a, b))
    return (basis, gram_y)


def solution(mesh):
    placed = (P("gx", None, "yz"), P())
    return jax.shard_map(
        on_device, mesh=mesh, in_specs=placed, out_specs=(P(), P("yz", "gx")), check_vma=False
    )
```

```python
import functools
import math

import jax
import jax.numpy as jnp
from jax import lax
from jax.experimental import pallas as pl
from jax.experimental.pallas import tpu as pltpu
from jax.sharding import PartitionSpec as P

ITERS = 4
WINDOW = 8
AHEAD = 0
LATE = 1
TALL = 8
LINE = 4
MIB = 1024 * 1024
F32 = jnp.float32
BF16 = jnp.bfloat16


def halves(value):
    high = value.astype(BF16)
    low = (value - high.astype(F32)).astype(BF16)
    return high, low


def dot_nt(left, right):
    return lax.dot_general(left, right, (((1,), (1,)), ((), ())), preferred_element_type=F32)


def dot_tn(left, right):
    return lax.dot_general(left, right, (((0,), (0,)), ((), ())), preferred_element_type=F32)


def gram_body(steps, slab_ref, before_ref, out_ref, main, cross):
    step = pl.program_id(0)

    @pl.when(step == 0)
    def _():
        main[...] = jnp.zeros_like(main)
        cross[...] = jnp.zeros_like(cross)

    depth = slab_ref.shape[0]
    parts = [halves(slab_ref[z]) for z in range(depth)]
    high = jnp.concatenate([part[0] for part in parts], axis=1)
    low = jnp.concatenate([part[1] for part in parts], axis=1)
    main[...] += dot_nt(high, high)
    cross[...] += dot_nt(high, low)

    @pl.when(step == steps - 1)
    def _():
        mixed = cross[...]
        out_ref[...] = before_ref[...] + main[...] + mixed + mixed.T


def gram_of(slab, before):
    depth, width_x, width_y = slab.shape
    block = 4 if depth % 4 == 0 else 1
    steps = depth // block
    square = pl.BlockSpec((width_x, width_x), lambda i: (0, 0))
    return pl.pallas_call(
        functools.partial(gram_body, steps),
        grid=(steps,),
        in_specs=[pl.BlockSpec((block, width_x, width_y), lambda i: (i, 0, 0)), square],
        out_specs=square,
        out_shape=jax.ShapeDtypeStruct((width_x, width_x), F32),
        scratch_shapes=[pltpu.VMEM((width_x, width_x), F32)] * 2,
        compiler_params=pltpu.CompilerParams(vmem_limit_bytes=32 * MIB),
        cost_estimate=pl.CostEstimate(
            flops=4 * width_x * width_x * depth * width_y,
            bytes_accessed=slab.size * 4,
            transcendentals=0,
        ),
        name="gram_x",
    )(slab, before)


def core_body(steps, total, field_ref, basis_ref, out_ref, stacked_ref, high_ref, low_ref, main, cross):
    step = pl.program_id(0)
    rank = basis_ref.shape[1]

    @pl.when(step == 0)
    def _():
        main[...] = jnp.zeros_like(main)
        cross[...] = jnp.zeros_like(cross)
        basis_high, basis_low = halves(basis_ref[...].T)
        stacked_ref[:rank] = basis_high
        stacked_ref[rank:] = basis_low

    blocks, depth, _, width = field_ref.shape
    stacked = stacked_ref[...]
    for z in range(depth):
        for b in range(blocks):
            high, low = halves(field_ref[b, z])
            both = jnp.dot(stacked, high, preferred_element_type=F32)
            core = both[:rank] + both[rank:]
            core += jnp.dot(stacked[:rank], low, preferred_element_type=F32)
            core_high, core_low = halves(core)
            high_ref[pl.ds(z * rank, rank), pl.ds(b * width, width)] = core_high
            low_ref[pl.ds(z * rank, rank), pl.ds(b * width, width)] = core_low
    high = high_ref[...]
    main[...] += dot_tn(high, high)
    cross[...] += dot_tn(high, low_ref[...])

    @pl.when(step == steps - 1)
    def _():
        mixed = cross[...]
        out_ref[...] = (main[...] + mixed + mixed.T) / total


def core_gram(cells, basis, total):
    blocks, depth, width_x, width = cells.shape
    rank = basis.shape[1]
    width_y = blocks * width
    block = 2 if depth % 2 == 0 else 1
    steps = depth // block
    return pl.pallas_call(
        functools.partial(core_body, steps, total),
        grid=(steps,),
        in_specs=[
            pl.BlockSpec((blocks, block, width_x, width), lambda i: (0, i, 0, 0)),
            pl.BlockSpec((width_x, rank), lambda i: (0, 0)),
        ],
        out_specs=pl.BlockSpec((width_y, width_y), lambda i: (0, 0)),
        out_shape=jax.ShapeDtypeStruct((width_y, width_y), F32),
        scratch_shapes=[
            pltpu.VMEM((2 * rank, width_x), BF16),
            pltpu.VMEM((block * rank, width_y), BF16),
            pltpu.VMEM((block * rank, width_y), BF16),
            pltpu.VMEM((width_y, width_y), F32),
            pltpu.VMEM((width_y, width_y), F32),
        ],
        compiler_params=pltpu.CompilerParams(vmem_limit_bytes=48 * MIB),
        cost_estimate=pl.CostEstimate(
            flops=6 * rank * cells.size + 4 * rank * depth * width_y * width_y,
            bytes_accessed=cells.size * 4,
            transcendentals=0,
        ),
        name="core_gram_y",
    )(cells, basis)


def full_dot(left, right, contract):
    return lax.dot_general(
        left,
        right,
        ((contract[:1], contract[1:]), ((), ())),
        precision=lax.Precision.HIGHEST,
        preferred_element_type=F32,
    )


def inverse_factor(cross):
    size = cross.shape[0]
    wide = 4
    groups = size // TALL
    shape = (TALL, size)
    sublane = lax.broadcasted_iota(jnp.int32, shape, 0)
    lane = lax.broadcasted_iota(jnp.int32, shape, 1)
    left = [cross[t * TALL : (t + 1) * TALL] for t in range(groups)]
    right = [(lane == sublane + t * TALL).astype(F32) for t in range(groups)]
    pivots = [jnp.ones(shape, F32) for _ in range(groups)]
    ratios = [jnp.zeros(shape, F32) for _ in range(groups)]

    def row(value, s):
        return jnp.broadcast_to(value[s : s + 1, :], shape)

    for first in range(0, size, wide):
        top, s0 = first // TALL, first % TALL
        below = range(top, groups)
        columns = [
            {t: jnp.broadcast_to(left[t][:, first + k : first + k + 1], shape) for t in below}
            for k in range(wide)
        ]
        rows = [row(left[top], s0 + k) for k in range(wide)]
        eyes = [row(right[top], s0 + k) for k in range(wide)]
        for i in range(0, wide, 2):
            a = row(columns[i][top], s0 + i)
            b = row(columns[i][top], s0 + i + 1)
            c = row(columns[i + 1][top], s0 + i + 1)
            inverse = 1.0 / (a * c - b * b)
            solved = (
                (rows[i] * c - rows[i + 1] * b) * inverse,
                (rows[i + 1] * a - rows[i] * b) * inverse,
                (eyes[i] * c - eyes[i + 1] * b) * inverse,
                (eyes[i + 1] * a - eyes[i] * b) * inverse,
            )
            ratio = b / a
            pivots[top] = jnp.where(sublane == s0 + i, a, pivots[top])
            pivots[top] = jnp.where(sublane == s0 + i + 1, c - b * ratio, pivots[top])
            ratios[top] = jnp.where(sublane == s0 + i + 1, ratio, ratios[top])
            for k in range(i + 2, wide):
                one, two = (row(columns[j][top], s0 + k) for j in (i, i + 1))
                first_part = (one * c - two * b) * inverse
                second_part = (two * a - one * b) * inverse
                for t in below:
                    columns[k][t] = columns[k][t] - (
                        first_part * columns[i][t] + second_part * columns[i + 1][t]
                    )
                rows[k] = rows[k] - (first_part * rows[i] + second_part * rows[i + 1])
                eyes[k] = eyes[k] - (first_part * eyes[i] + second_part * eyes[i + 1])
            rest = sublane >= s0 + wide
            for t in below:
                one, two = columns[i][t], columns[i + 1][t]
                new_left = left[t] - (one * solved[0] + two * solved[1])
                new_right = right[t] - (one * solved[2] + two * solved[3])
                if t == top:
                    new_left = jnp.where(rest, new_left, left[t])
                    new_right = jnp.where(rest, new_right, right[t])
                    for j in (i, i + 1):
                        new_right = jnp.where(sublane == s0 + j, eyes[j], new_right)
                left[t], right[t] = new_left, new_right
    for t in range(groups):
        above = jnp.concatenate([right[t][:1], right[t][:-1]], axis=0)
        value = right[t] - ratios[t] * above
        root = lax.rsqrt(pivots[t])
        root = root * (1.5 - 0.5 * pivots[t] * root * root)
        right[t] = value * root
    return jnp.concatenate(right, axis=0)


def iterate_body(total, places_ref, *refs):
    *piece_refs, start_ref, out_ref, gram = refs
    height = piece_refs[0].shape[0]
    for i, piece_ref in enumerate(piece_refs):
        place = pl.multiple_of(places_ref[i] * height, height)
        gram[pl.ds(place, height)] = piece_ref[...] / total
    out_ref[...] = start_ref[...]

    def step(_, carry):
        product = full_dot(gram[...], out_ref[...], (1, 0))
        product = product * lax.rsqrt(jnp.sum(product * product, axis=0, keepdims=True))
        inverse = inverse_factor(full_dot(product, product, (0, 0)))
        out_ref[...] = full_dot(product, inverse, (1, 1))
        return carry

    lax.fori_loop(0, ITERS, step, 0)


def iterate(pieces, places, start, total):
    width_x, rank = start.shape
    return pl.pallas_call(
        functools.partial(iterate_body, total),
        in_specs=[pl.BlockSpec(memory_space=pltpu.SMEM)]
        + [pl.BlockSpec(memory_space=pltpu.VMEM)] * (len(pieces) + 1),
        out_specs=pl.BlockSpec(memory_space=pltpu.VMEM),
        out_shape=jax.ShapeDtypeStruct((width_x, rank), F32),
        scratch_shapes=[pltpu.VMEM((width_x, width_x), F32)],
        compiler_params=pltpu.CompilerParams(vmem_limit_bytes=24 * MIB),
        cost_estimate=pl.CostEstimate(
            flops=4 * 10**10, bytes_accessed=8 * start.size, transcendentals=0
        ),
        name="subspace",
    )(places, *pieces, start)


def stack_body(places_ref, *refs):
    *piece_refs, out_ref = refs
    for i, piece_ref in enumerate(piece_refs):
        out_ref[places_ref[i]] = piece_ref[...]


def stack(pieces, places):
    return pl.pallas_call(
        stack_body,
        in_specs=[pl.BlockSpec(memory_space=pltpu.SMEM)]
        + [pl.BlockSpec(memory_space=pltpu.VMEM)] * len(pieces),
        out_specs=pl.BlockSpec(memory_space=pltpu.VMEM),
        out_shape=jax.ShapeDtypeStruct((len(pieces),) + pieces[0].shape, F32),
        compiler_params=pltpu.CompilerParams(vmem_limit_bytes=16 * MIB),
        name="stack_rows",
    )(places, *pieces)


def pack_body(first_ref, field_ref, out_ref):
    for z in range(field_ref.shape[1]):
        out_ref[z] = field_ref[:, z, :]


def pack(field, first, depth):
    x_block, _, y_block = field.shape
    return pl.pallas_call(
        pack_body,
        grid_spec=pltpu.PrefetchScalarGridSpec(
            num_scalar_prefetch=1,
            grid=(depth // TALL,),
            in_specs=[pl.BlockSpec((x_block, TALL, y_block), lambda i, at: (0, at[0] + i, 0))],
            out_specs=pl.BlockSpec((TALL, x_block, y_block), lambda i, at: (i, 0, 0)),
        ),
        out_shape=jax.ShapeDtypeStruct((depth, x_block, y_block), F32),
        compiler_params=pltpu.CompilerParams(vmem_limit_bytes=48 * MIB),
        cost_estimate=pl.CostEstimate(
            flops=0, bytes_accessed=1, transcendentals=0
        ),
        name="pack_z",
    )(first.astype(jnp.int32).reshape(1), field)


def tie(value, others):
    return lax.optimization_barrier((value, *others))[0] if others else value


class Line:
    def __init__(self):
        self.ends = []

    def done(self, ahead):
        last = len(self.ends) - WINDOW + 1 - ahead
        return self.ends[max(0, last - 1) : max(0, last)]

    def send(self, cut, index, axis, perm, after=()):
        value = cut(tie(index, self.done(AHEAD)))
        got = lax.ppermute(tie(value, self.done(0) + list(after)), axis, perm)
        self.ends.append(got)
        return got


def chunk_depths(groups):
    if groups < 4:
        return [groups]
    last = max(1, groups // 8)
    left = groups - 2 * last
    first = [(left + k) // 3 for k in (2, 1, 0)]
    return [depth for depth in first if depth] + [last, last]


def on_device(field, start):
    n = lax.axis_size("gx")
    m = lax.axis_size("yz")
    g = lax.axis_index("gx")
    q = lax.axis_index("yz")
    x_block, depth, y_block = field.shape
    width_x, width_y = x_block * n, y_block * m
    rank = start.shape[1]
    slab = depth // n
    line = LINE if n % LINE == 0 else 1
    rest = n // line
    order = Line()

    def moved(index, a, b, sign=1):
        return (index // rest + sign * a) % line * rest + (index % rest + sign * b) % rest

    def gx_perm(a, b):
        return [(i, moved(i, a, b)) for i in range(n)]

    def yz_perm(d):
        return [(i, (i + d) % m) for i in range(m)]

    far = sorted(range(1, line), key=lambda a: abs(2 * a - line))
    shifts = [(a, (b + k) % rest) for b in range(rest) for k, a in enumerate(far)]
    shifts[4:4] = [(0, b) for b in range(1, rest)]
    turns = sorted(range(1, m), key=lambda d: abs(2 * d - m))

    cells = jnp.zeros((m, slab // m, width_x, y_block), F32)

    def to_gx(first, zc, a, b, whole, after):
        place = (moved(g, a, b) * slab + first) // TALL
        got = order.send(lambda at: pack(field, at, zc), place, "gx", gx_perm(a, b), after)
        return lax.dynamic_update_slice_in_dim(whole, got[:, None], moved(g, a, b, -1), axis=1)

    cores = 2 if m % 2 == 0 else 1
    chips = m // cores
    core, chip = q % cores, q // cores

    def core_perm(d):
        return [(i, i // cores * cores + (i + d) % cores) for i in range(m)]

    def chip_perm(d):
        return [(i, (i + d * cores) % m) for i in range(m)]

    def part(array, index, count):
        depth = array.shape[0] // count
        return lax.dynamic_slice_in_dim(array, index * depth, depth, axis=0)

    def to_core(whole):
        both = jnp.zeros((cores, whole.shape[0] // cores, width_x, y_block), F32)
        own = part(whole, core, cores)[None]
        both = lax.dynamic_update_slice_in_dim(both, own, core, axis=0)
        for d in range(1, cores):
            cut = part(whole, (core + d) % cores, cores)
            got = lax.ppermute(cut, "yz", core_perm(d))
            both = lax.dynamic_update_slice_in_dim(both, got[None], (core - d) % cores, axis=0)
        return both

    def to_chip(cells, first, both, after):
        zs = both.shape[1] // chips

        def put(cells, value, source):
            return lax.dynamic_update_slice(cells, value, (source * cores, first // m, 0, 0))

        def cut(array, index):
            return lax.dynamic_slice_in_dim(array, index * zs, zs, axis=1)

        cells = put(cells, cut(both, chip), chip)
        for d in range(1, chips):
            got = lax.ppermute(cut(tie(both, after), (chip + d) % chips), "yz", chip_perm(d))
            cells = put(cells, got, (chip - d) % chips)
        return cells

    def to_yz(cells, first, whole):
        parts = whole.reshape(m, whole.shape[0] // m, width_x, y_block)
        got = lax.all_to_all(parts, "yz", split_axis=0, concat_axis=0)
        return lax.dynamic_update_slice_in_dim(cells, got, first // m, axis=1), got

    gram = jnp.zeros((width_x, width_x), F32)
    before, start_z, first, across = None, 0, 0, None
    group = math.lcm(m, TALL)
    for groups in chunk_depths(slab // group):
        zc = groups * group
        whole = jnp.zeros((zc, n, x_block, y_block), F32)
        for k, (a, b) in enumerate(shifts):
            after = [across] if before is not None and k == len(shifts) - 1 else []
            whole = to_gx(first, zc, a, b, whole, after)
            if before is not None and k == LATE:
                cells, across = to_yz(cells, start_z, tie(before, [order.ends[-1]]))
        own = pack(field, (g * slab + first) // TALL, zc)[:, None]
        whole = lax.dynamic_update_slice_in_dim(whole, own, g, axis=1)
        before = whole.reshape(zc, width_x, y_block)
        gram = gram_of(before, gram)
        start_z, first = first, first + zc

    rows = width_x // m
    both = to_core(before)
    slabs = gram.reshape(m, rows, width_x)

    def pick(array, index):
        return lax.dynamic_index_in_dim(array, index, axis=0, keepdims=False)

    summed = pick(slabs, q)
    for d in turns:
        summed = summed + lax.ppermute(pick(slabs, (q + d) % m), "yz", yz_perm(d))
    cells = to_chip(cells, start_z, both, [summed])
    strips = summed.reshape(n, rows // n, width_x)
    summed = pick(strips, g)
    for a, b in shifts:
        summed = summed + lax.ppermute(pick(strips, moved(g, a, b)), "gx", gx_perm(a, b))
    pieces = [summed] + [lax.ppermute(summed, "gx", gx_perm(a, b)) for a, b in shifts]
    places = jnp.stack([g] + [moved(g, a, b, -1) for a, b in shifts]).astype(jnp.int32)
    summed = stack(pieces, places).reshape(rows, width_x)
    pieces = [summed] + [lax.ppermute(summed, "yz", yz_perm(d)) for d in turns]
    places = jnp.stack([q] + [(q - d) % m for d in turns]).astype(jnp.int32)
    basis = iterate(pieces, places, start, float(width_y * depth))

    partial_y = core_gram(cells, basis, float(rank * depth))
    blocks = partial_y.reshape(chips, cores, y_block, width_y)

    def of_core(index):
        return lax.dynamic_index_in_dim(blocks, index, axis=1, keepdims=False)

    blocks_here = of_core(core)
    for d in range(1, cores):
        blocks_here = blocks_here + lax.ppermute(
            of_core((core + d) % cores), "yz", core_perm(d)
        )
    rows_y = pick(blocks_here, chip)
    for d in range(1, chips):
        rows_y = rows_y + lax.ppermute(
            pick(blocks_here, (chip + d) % chips), "yz", chip_perm(d)
        )
    width = width_y // n

    def block(index):
        return lax.dynamic_slice_in_dim(rows_y, index * width, width, axis=1)

    gram_y = block(g)
    for a, b in shifts:
        gram_y = gram_y + lax.ppermute(block(moved(g, a, b)), "gx", gx_perm(a, b))
    return (basis, gram_y)


def solution(mesh):
    placed = (P("gx", None, "yz"), P())
    return jax.shard_map(
        on_device, mesh=mesh, in_specs=placed, out_specs=(P(), P("yz", "gx")), check_vma=False
    )
```

```python
import functools
import math

import jax
import jax.numpy as jnp
from jax import lax
from jax.experimental import pallas as pl
from jax.experimental.pallas import tpu as pltpu
from jax.sharding import PartitionSpec as P

ITERS = 4
WINDOW = 5
AHEAD = 2
TALL = 8
LINE = 4
MIB = 1024 * 1024
F32 = jnp.float32
BF16 = jnp.bfloat16


def halves(value):
    high = value.astype(BF16)
    low = (value - high.astype(F32)).astype(BF16)
    return high, low


def dot_nt(left, right):
    return lax.dot_general(left, right, (((1,), (1,)), ((), ())), preferred_element_type=F32)


def dot_tn(left, right):
    return lax.dot_general(left, right, (((0,), (0,)), ((), ())), preferred_element_type=F32)


def gram_body(steps, slab_ref, before_ref, out_ref, main, cross):
    step = pl.program_id(0)

    @pl.when(step == 0)
    def _():
        main[...] = jnp.zeros_like(main)
        cross[...] = jnp.zeros_like(cross)

    depth = slab_ref.shape[0]
    parts = [halves(slab_ref[z]) for z in range(depth)]
    high = jnp.concatenate([part[0] for part in parts], axis=1)
    low = jnp.concatenate([part[1] for part in parts], axis=1)
    main[...] += dot_nt(high, high)
    cross[...] += dot_nt(high, low)

    @pl.when(step == steps - 1)
    def _():
        mixed = cross[...]
        out_ref[...] = before_ref[...] + main[...] + mixed + mixed.T


def gram_of(slab, before):
    depth, width_x, width_y = slab.shape
    block = 4 if depth % 4 == 0 else 1
    steps = depth // block
    square = pl.BlockSpec((width_x, width_x), lambda i: (0, 0))
    return pl.pallas_call(
        functools.partial(gram_body, steps),
        grid=(steps,),
        in_specs=[pl.BlockSpec((block, width_x, width_y), lambda i: (i, 0, 0)), square],
        out_specs=square,
        out_shape=jax.ShapeDtypeStruct((width_x, width_x), F32),
        scratch_shapes=[pltpu.VMEM((width_x, width_x), F32)] * 2,
        compiler_params=pltpu.CompilerParams(vmem_limit_bytes=32 * MIB),
        cost_estimate=pl.CostEstimate(
            flops=4 * width_x * width_x * depth * width_y,
            bytes_accessed=slab.size * 4,
            transcendentals=0,
        ),
        name="gram_x",
    )(slab, before)


def core_body(steps, total, field_ref, basis_ref, out_ref, stacked_ref, high_ref, low_ref, main, cross):
    step = pl.program_id(0)
    rank = basis_ref.shape[1]

    @pl.when(step == 0)
    def _():
        main[...] = jnp.zeros_like(main)
        cross[...] = jnp.zeros_like(cross)
        basis_high, basis_low = halves(basis_ref[...].T)
        stacked_ref[:rank] = basis_high
        stacked_ref[rank:] = basis_low

    depth, blocks, _, width = field_ref.shape
    stacked = stacked_ref[...]
    for z in range(depth):
        for b in range(blocks):
            high, low = halves(field_ref[z, b])
            both = jnp.dot(stacked, high, preferred_element_type=F32)
            core = both[:rank] + both[rank:]
            core += jnp.dot(stacked[:rank], low, preferred_element_type=F32)
            core_high, core_low = halves(core)
            high_ref[pl.ds(z * rank, rank), pl.ds(b * width, width)] = core_high
            low_ref[pl.ds(z * rank, rank), pl.ds(b * width, width)] = core_low
    high = high_ref[...]
    main[...] += dot_tn(high, high)
    cross[...] += dot_tn(high, low_ref[...])

    @pl.when(step == steps - 1)
    def _():
        mixed = cross[...]
        out_ref[...] = (main[...] + mixed + mixed.T) / total


def core_gram(cells, basis, total):
    depth, blocks, width_x, width = cells.shape
    rank = basis.shape[1]
    width_y = blocks * width
    block = 2 if depth % 2 == 0 else 1
    steps = depth // block
    return pl.pallas_call(
        functools.partial(core_body, steps, total),
        grid=(steps,),
        in_specs=[
            pl.BlockSpec((block, blocks, width_x, width), lambda i: (i, 0, 0, 0)),
            pl.BlockSpec((width_x, rank), lambda i: (0, 0)),
        ],
        out_specs=pl.BlockSpec((width_y, width_y), lambda i: (0, 0)),
        out_shape=jax.ShapeDtypeStruct((width_y, width_y), F32),
        scratch_shapes=[
            pltpu.VMEM((2 * rank, width_x), BF16),
            pltpu.VMEM((block * rank, width_y), BF16),
            pltpu.VMEM((block * rank, width_y), BF16),
            pltpu.VMEM((width_y, width_y), F32),
            pltpu.VMEM((width_y, width_y), F32),
        ],
        compiler_params=pltpu.CompilerParams(vmem_limit_bytes=48 * MIB),
        cost_estimate=pl.CostEstimate(
            flops=6 * rank * cells.size + 4 * rank * depth * width_y * width_y,
            bytes_accessed=cells.size * 4,
            transcendentals=0,
        ),
        name="core_gram_y",
    )(cells, basis)


def full_dot(left, right, contract):
    return lax.dot_general(
        left,
        right,
        ((contract[:1], contract[1:]), ((), ())),
        precision=lax.Precision.HIGHEST,
        preferred_element_type=F32,
    )


def inverse_factor(cross):
    size = cross.shape[0]
    tall = 8
    wide = 4
    groups = size // tall
    shape = (tall, size)
    sublane = lax.broadcasted_iota(jnp.int32, shape, 0)
    lane = lax.broadcasted_iota(jnp.int32, shape, 1)
    left = [cross[t * tall : (t + 1) * tall] for t in range(groups)]
    right = [(lane == sublane + t * tall).astype(F32) for t in range(groups)]
    pivots = [jnp.ones(shape, F32) for _ in range(groups)]

    def row(value, s):
        return jnp.broadcast_to(value[s : s + 1, :], shape)

    for first in range(0, size, wide):
        top, s0 = first // tall, first % tall
        below = range(top, groups)
        columns = [
            {t: jnp.broadcast_to(left[t][:, first + k : first + k + 1], shape) for t in below}
            for k in range(wide)
        ]
        rows = [row(left[top], s0 + k) for k in range(wide)]
        eyes = [row(right[top], s0 + k) for k in range(wide)]
        scaled = []
        for i in range(wide):
            pivot = row(columns[i][top], s0 + i)
            inverse = 1.0 / pivot
            scaled.append((rows[i] * inverse, eyes[i] * inverse))
            for k in range(i + 1, wide):
                ratio = row(columns[i][top], s0 + k) * inverse
                for t in below:
                    columns[k][t] = columns[k][t] - ratio * columns[i][t]
                rows[k] = rows[k] - ratio * rows[i]
                eyes[k] = eyes[k] - ratio * eyes[i]
            here = sublane == s0 + i
            pivots[top] = jnp.where(here, pivot, pivots[top])
        rest = sublane >= s0 + wide
        for t in below:
            new_left, new_right = left[t], right[t]
            for i in range(wide):
                new_left = new_left - columns[i][t] * scaled[i][0]
                new_right = new_right - columns[i][t] * scaled[i][1]
            if t == top:
                new_left = jnp.where(rest, new_left, left[t])
                new_right = jnp.where(rest, new_right, right[t])
                for i in range(wide):
                    new_right = jnp.where(sublane == s0 + i, eyes[i], new_right)
            left[t], right[t] = new_left, new_right
    for t in range(groups):
        root = lax.rsqrt(pivots[t])
        root = root * (1.5 - 0.5 * pivots[t] * root * root)
        right[t] = right[t] * root
    return jnp.concatenate(right, axis=0)


def iterate_body(total, places_ref, *refs):
    *piece_refs, start_ref, out_ref, gram = refs
    height = piece_refs[0].shape[0]
    for i, piece_ref in enumerate(piece_refs):
        place = pl.multiple_of(places_ref[i] * height, height)
        gram[pl.ds(place, height)] = piece_ref[...] / total
    out_ref[...] = start_ref[...]

    def step(_, carry):
        product = full_dot(gram[...], out_ref[...], (1, 0))
        inverse = inverse_factor(full_dot(product, product, (0, 0)))
        out_ref[...] = full_dot(product, inverse, (1, 1))
        return carry

    lax.fori_loop(0, ITERS, step, 0)


def iterate(pieces, places, start, total):
    width_x, rank = start.shape
    return pl.pallas_call(
        functools.partial(iterate_body, total),
        in_specs=[pl.BlockSpec(memory_space=pltpu.SMEM)]
        + [pl.BlockSpec(memory_space=pltpu.VMEM)] * (len(pieces) + 1),
        out_specs=pl.BlockSpec(memory_space=pltpu.VMEM),
        out_shape=jax.ShapeDtypeStruct((width_x, rank), F32),
        scratch_shapes=[pltpu.VMEM((width_x, width_x), F32)],
        compiler_params=pltpu.CompilerParams(vmem_limit_bytes=24 * MIB),
        cost_estimate=pl.CostEstimate(
            flops=4 * 10**10, bytes_accessed=8 * start.size, transcendentals=0
        ),
        name="subspace",
    )(places, *pieces, start)


def stack_body(places_ref, *refs):
    *piece_refs, out_ref = refs
    for i, piece_ref in enumerate(piece_refs):
        out_ref[places_ref[i]] = piece_ref[...]


def stack(pieces, places):
    return pl.pallas_call(
        stack_body,
        in_specs=[pl.BlockSpec(memory_space=pltpu.SMEM)]
        + [pl.BlockSpec(memory_space=pltpu.VMEM)] * len(pieces),
        out_specs=pl.BlockSpec(memory_space=pltpu.VMEM),
        out_shape=jax.ShapeDtypeStruct((len(pieces),) + pieces[0].shape, F32),
        compiler_params=pltpu.CompilerParams(vmem_limit_bytes=16 * MIB),
        name="stack_rows",
    )(places, *pieces)


def pack_body(first_ref, field_ref, out_ref):
    for z in range(field_ref.shape[1]):
        out_ref[z] = field_ref[:, z, :]


def pack(field, first, depth):
    x_block, _, y_block = field.shape
    return pl.pallas_call(
        pack_body,
        grid_spec=pltpu.PrefetchScalarGridSpec(
            num_scalar_prefetch=1,
            grid=(depth // TALL,),
            in_specs=[pl.BlockSpec((x_block, TALL, y_block), lambda i, at: (0, at[0] + i, 0))],
            out_specs=pl.BlockSpec((TALL, x_block, y_block), lambda i, at: (i, 0, 0)),
        ),
        out_shape=jax.ShapeDtypeStruct((depth, x_block, y_block), F32),
        compiler_params=pltpu.CompilerParams(vmem_limit_bytes=48 * MIB),
        cost_estimate=pl.CostEstimate(
            flops=0, bytes_accessed=8 * depth * x_block * y_block, transcendentals=0
        ),
        name="pack_z",
    )(first.astype(jnp.int32).reshape(1), field)


def tie(value, others):
    return lax.optimization_barrier((value, *others))[0] if others else value


class Line:
    def __init__(self):
        self.ends = []

    def done(self, ahead):
        last = len(self.ends) - WINDOW + 1 - ahead
        return self.ends[max(0, last - 1) : max(0, last)]

    def send(self, cut, source, axis, perm):
        value = cut(tie(source, self.done(AHEAD)))
        got = lax.ppermute(tie(value, self.done(0)), axis, perm)
        self.ends.append(got)
        return got


def chunk_depths(groups):
    if groups < 4:
        return [groups]
    last = max(1, groups // 8)
    left = groups - 2 * last
    first = [(left + k) // 3 for k in (2, 1, 0)]
    return [depth for depth in first if depth] + [last, last]


def on_device(field, start):
    n = lax.axis_size("gx")
    m = lax.axis_size("yz")
    g = lax.axis_index("gx")
    q = lax.axis_index("yz")
    x_block, depth, y_block = field.shape
    width_x, width_y = x_block * n, y_block * m
    rank = start.shape[1]
    slab = depth // n
    line = LINE if n % LINE == 0 else 1
    rest = n // line
    order = Line()

    def moved(index, a, b, sign=1):
        return (index // rest + sign * a) % line * rest + (index % rest + sign * b) % rest

    def gx_perm(a, b):
        return [(i, moved(i, a, b)) for i in range(n)]

    def yz_perm(d):
        return [(i, (i + d) % m) for i in range(m)]

    far = sorted(range(1, line), key=lambda a: abs(2 * a - line))
    shifts = [(a, (b + k) % rest) for b in range(rest) for k, a in enumerate(far)]
    shifts[4:4] = [(0, b) for b in range(1, rest)]
    turns = sorted(range(1, m), key=lambda d: abs(2 * d - m))

    cells = jnp.zeros((slab // m, m, width_x, y_block), F32)

    def to_gx(first, zc, a, b, whole):
        place = (moved(g, a, b) * slab + first) // TALL
        got = order.send(lambda at: pack(field, at, zc), place, "gx", gx_perm(a, b))
        return lax.dynamic_update_slice_in_dim(whole, got[:, None], moved(g, a, b, -1), axis=1)

    def to_yz(cells, first, d, whole, after=()):
        zs = whole.shape[0] // m

        def cut(source):
            return lax.dynamic_slice_in_dim(source, (q + d) % m * zs, zs, axis=0)

        got = order.send(cut, tie(whole, after), "yz", yz_perm(d))
        return lax.dynamic_update_slice(cells, got[:, None], (first // m, (q - d) % m, 0, 0))

    gram = jnp.zeros((width_x, width_x), F32)
    first, waiting = 0, []
    group = math.lcm(m, TALL)
    for groups in chunk_depths(slab // group):
        zc = groups * group
        units = zc // m
        whole = jnp.zeros((zc, n, x_block, y_block), F32)
        for k, (a, b) in enumerate(shifts):
            whole = to_gx(first, zc, a, b, whole)
            if k % 3 == 1 or k == len(shifts) - 1:
                if waiting and (k >= WINDOW - 1 or len(waiting) > len(turns)):
                    cells = to_yz(cells, *waiting.pop(0))
        own = pack(field, (g * slab + first) // TALL, zc)[:, None]
        whole = lax.dynamic_update_slice_in_dim(whole, own, g, axis=1)
        before = whole.reshape(zc, width_x, y_block)
        gram = gram_of(before, gram)
        own = lax.dynamic_slice_in_dim(before, q * units, units, axis=0)
        cells = lax.dynamic_update_slice(cells, own[:, None], (first // m, q, 0, 0))
        waiting += [(first, d, before) for d in turns]
        first += zc

    rows = width_x // m
    slabs = gram.reshape(m, rows, width_x)

    def pick(array, index):
        return lax.dynamic_index_in_dim(array, index, axis=0, keepdims=False)

    summed = pick(slabs, q)
    for d in turns:
        summed = summed + lax.ppermute(pick(slabs, (q + d) % m), "yz", yz_perm(d))
    while len(waiting) >= len(turns):
        cells = to_yz(cells, *waiting.pop(0), [summed])
    strips = summed.reshape(n, rows // n, width_x)
    summed = pick(strips, g)
    for a, b in shifts:
        summed = summed + lax.ppermute(pick(strips, moved(g, a, b)), "gx", gx_perm(a, b))
    pieces = [summed] + [lax.ppermute(summed, "gx", gx_perm(a, b)) for a, b in shifts]
    places = jnp.stack([g] + [moved(g, a, b, -1) for a, b in shifts]).astype(jnp.int32)
    summed = stack(pieces, places).reshape(rows, width_x)
    pieces = [summed] + [lax.ppermute(summed, "yz", yz_perm(d)) for d in turns]
    places = jnp.stack([q] + [(q - d) % m for d in turns]).astype(jnp.int32)
    for entry in waiting:
        cells = to_yz(cells, *entry, pieces[1:])
    basis = iterate(pieces, places, start, float(width_y * depth))

    partial_y = core_gram(cells, basis, float(rank * depth))
    cores = 2 if m % 2 == 0 else 1
    chips = m // cores
    core, chip = q % cores, q // cores
    blocks = partial_y.reshape(chips, cores, y_block, width_y)

    def of_core(index):
        return lax.dynamic_index_in_dim(blocks, index, axis=1, keepdims=False)

    blocks_here = of_core(core)
    for d in range(1, cores):
        perm = [(i, i // cores * cores + (i + d) % cores) for i in range(m)]
        blocks_here = blocks_here + lax.ppermute(of_core((core + d) % cores), "yz", perm)
    rows_y = pick(blocks_here, chip)
    for d in range(1, chips):
        perm = [(i, (i + d * cores) % m) for i in range(m)]
        rows_y = rows_y + lax.ppermute(pick(blocks_here, (chip + d) % chips), "yz", perm)
    width = width_y // n

    def block(index):
        return lax.dynamic_slice_in_dim(rows_y, index * width, width, axis=1)

    gram_y = block(g)
    for a, b in shifts:
        gram_y = gram_y + lax.ppermute(block(moved(g, a, b)), "gx", gx_perm(a, b))
    return (basis, gram_y)


def solution(mesh):
    placed = (P("gx", None, "yz"), P())
    return jax.shard_map(
        on_device, mesh=mesh, in_specs=placed, out_specs=(P(), P("yz", "gx")), check_vma=False
    )
```

```python
import functools
import math

import jax
import jax.numpy as jnp
from jax import lax
from jax.experimental import pallas as pl
from jax.experimental.pallas import tpu as pltpu
from jax.sharding import PartitionSpec as P

ITERS = 4
WINDOW = 5
AHEAD = 2
TALL = 8
LINE = 4
MIB = 1024 * 1024
F32 = jnp.float32
BF16 = jnp.bfloat16


def halves(value):
    high = value.astype(BF16)
    low = (value - high.astype(F32)).astype(BF16)
    return high, low


def dot_nt(left, right):
    return lax.dot_general(left, right, (((1,), (1,)), ((), ())), preferred_element_type=F32)


def dot_tn(left, right):
    return lax.dot_general(left, right, (((0,), (0,)), ((), ())), preferred_element_type=F32)


def gram_body(steps, slab_ref, before_ref, out_ref, main, cross):
    step = pl.program_id(0)

    @pl.when(step == 0)
    def _():
        main[...] = jnp.zeros_like(main)
        cross[...] = jnp.zeros_like(cross)

    depth = slab_ref.shape[0]
    parts = [halves(slab_ref[z]) for z in range(depth)]
    high = jnp.concatenate([part[0] for part in parts], axis=1)
    low = jnp.concatenate([part[1] for part in parts], axis=1)
    main[...] += dot_nt(high, high)
    cross[...] += dot_nt(high, low)

    @pl.when(step == steps - 1)
    def _():
        mixed = cross[...]
        out_ref[...] = before_ref[...] + main[...] + mixed + mixed.T


def gram_of(slab, before):
    depth, width_x, width_y = slab.shape
    block = 4 if depth % 4 == 0 else 1
    steps = depth // block
    square = pl.BlockSpec((width_x, width_x), lambda i: (0, 0))
    return pl.pallas_call(
        functools.partial(gram_body, steps),
        grid=(steps,),
        in_specs=[pl.BlockSpec((block, width_x, width_y), lambda i: (i, 0, 0)), square],
        out_specs=square,
        out_shape=jax.ShapeDtypeStruct((width_x, width_x), F32),
        scratch_shapes=[pltpu.VMEM((width_x, width_x), F32)] * 2,
        compiler_params=pltpu.CompilerParams(vmem_limit_bytes=32 * MIB),
        cost_estimate=pl.CostEstimate(
            flops=4 * width_x * width_x * depth * width_y,
            bytes_accessed=slab.size * 4,
            transcendentals=0,
        ),
        name="gram_x",
    )(slab, before)


def core_body(steps, total, carried, field_ref, basis_ref, *refs):
    before, refs = refs[: 2 * carried], refs[2 * carried :]
    out_ref = refs[0] if total else None
    stacked_ref, high_ref, low_ref = refs[1:4] if total else refs[2:5]
    main, cross = refs[4:6] if total else refs[:2]
    step = pl.program_id(0)
    rank = basis_ref.shape[1]

    @pl.when(step == 0)
    def _():
        main[...] = before[0][...] if carried else jnp.zeros_like(main)
        cross[...] = before[1][...] if carried else jnp.zeros_like(cross)
        basis_high, basis_low = halves(basis_ref[...].T)
        stacked_ref[:rank] = basis_high
        stacked_ref[rank:] = basis_low

    depth, blocks, _, width = field_ref.shape
    stacked = stacked_ref[...]
    for z in range(depth):
        for b in range(blocks):
            high, low = halves(field_ref[z, b])
            both = jnp.dot(stacked, high, preferred_element_type=F32)
            core = both[:rank] + both[rank:]
            core += jnp.dot(stacked[:rank], low, preferred_element_type=F32)
            core_high, core_low = halves(core)
            high_ref[pl.ds(z * rank, rank), pl.ds(b * width, width)] = core_high
            low_ref[pl.ds(z * rank, rank), pl.ds(b * width, width)] = core_low
    high = high_ref[...]
    main[...] += dot_tn(high, high)
    cross[...] += dot_tn(high, low_ref[...])

    if total:

        @pl.when(step == steps - 1)
        def _():
            mixed = cross[...]
            out_ref[...] = (main[...] + mixed + mixed.T) / total


def core_gram(cells, basis, before=(), total=None):
    depth, blocks, width_x, width = cells.shape
    rank = basis.shape[1]
    width_y = blocks * width
    block = 2 if depth % 2 == 0 else 1
    steps = depth // block
    square = pl.BlockSpec((width_y, width_y), lambda i: (0, 0))
    shape = jax.ShapeDtypeStruct((width_y, width_y), F32)
    sums = [pltpu.VMEM((width_y, width_y), F32)] * 2
    return pl.pallas_call(
        functools.partial(core_body, steps, total, bool(before)),
        grid=(steps,),
        in_specs=[
            pl.BlockSpec((block, blocks, width_x, width), lambda i: (i, 0, 0, 0)),
            pl.BlockSpec((width_x, rank), lambda i: (0, 0)),
        ]
        + [square] * len(before),
        out_specs=square if total else [square] * 2,
        out_shape=shape if total else [shape] * 2,
        scratch_shapes=[
            pltpu.VMEM((2 * rank, width_x), BF16),
            pltpu.VMEM((block * rank, width_y), BF16),
            pltpu.VMEM((block * rank, width_y), BF16),
        ]
        + (sums if total else []),
        compiler_params=pltpu.CompilerParams(vmem_limit_bytes=52 * MIB),
        cost_estimate=pl.CostEstimate(
            flops=6 * rank * cells.size + 4 * rank * depth * width_y * width_y,
            bytes_accessed=cells.size * 4,
            transcendentals=0,
        ),
        name="core_gram_y",
    )(cells, basis, *before)


def full_dot(left, right, contract):
    return lax.dot_general(
        left,
        right,
        ((contract[:1], contract[1:]), ((), ())),
        precision=lax.Precision.HIGHEST,
        preferred_element_type=F32,
    )


def inverse_factor(cross):
    size = cross.shape[0]
    tall = 8
    wide = 4
    groups = size // tall
    shape = (tall, size)
    sublane = lax.broadcasted_iota(jnp.int32, shape, 0)
    lane = lax.broadcasted_iota(jnp.int32, shape, 1)
    left = [cross[t * tall : (t + 1) * tall] for t in range(groups)]
    right = [(lane == sublane + t * tall).astype(F32) for t in range(groups)]
    pivots = [jnp.ones(shape, F32) for _ in range(groups)]

    def row(value, s):
        return jnp.broadcast_to(value[s : s + 1, :], shape)

    for first in range(0, size, wide):
        top, s0 = first // tall, first % tall
        below = range(top, groups)
        columns = [
            {t: jnp.broadcast_to(left[t][:, first + k : first + k + 1], shape) for t in below}
            for k in range(wide)
        ]
        rows = [row(left[top], s0 + k) for k in range(wide)]
        eyes = [row(right[top], s0 + k) for k in range(wide)]
        scaled = []
        for i in range(wide):
            pivot = row(columns[i][top], s0 + i)
            inverse = 1.0 / pivot
            scaled.append((rows[i] * inverse, eyes[i] * inverse))
            for k in range(i + 1, wide):
                ratio = row(columns[i][top], s0 + k) * inverse
                for t in below:
                    columns[k][t] = columns[k][t] - ratio * columns[i][t]
                rows[k] = rows[k] - ratio * rows[i]
                eyes[k] = eyes[k] - ratio * eyes[i]
            here = sublane == s0 + i
            pivots[top] = jnp.where(here, pivot, pivots[top])
        rest = sublane >= s0 + wide
        for t in below:
            new_left, new_right = left[t], right[t]
            for i in range(wide):
                new_left = new_left - columns[i][t] * scaled[i][0]
                new_right = new_right - columns[i][t] * scaled[i][1]
            if t == top:
                new_left = jnp.where(rest, new_left, left[t])
                new_right = jnp.where(rest, new_right, right[t])
                for i in range(wide):
                    new_right = jnp.where(sublane == s0 + i, eyes[i], new_right)
            left[t], right[t] = new_left, new_right
    for t in range(groups):
        root = lax.rsqrt(pivots[t])
        root = root * (1.5 - 0.5 * pivots[t] * root * root)
        right[t] = right[t] * root
    return jnp.concatenate(right, axis=0)


def iterate_body(total, places_ref, *refs):
    *piece_refs, start_ref, out_ref, gram = refs
    height = piece_refs[0].shape[0]
    for i, piece_ref in enumerate(piece_refs):
        place = pl.multiple_of(places_ref[i] * height, height)
        gram[pl.ds(place, height)] = piece_ref[...] / total
    out_ref[...] = start_ref[...]

    def step(_, carry):
        product = full_dot(gram[...], out_ref[...], (1, 0))
        inverse = inverse_factor(full_dot(product, product, (0, 0)))
        out_ref[...] = full_dot(product, inverse, (1, 1))
        return carry

    lax.fori_loop(0, ITERS, step, 0)


def iterate(pieces, places, start, total):
    width_x, rank = start.shape
    return pl.pallas_call(
        functools.partial(iterate_body, total),
        in_specs=[pl.BlockSpec(memory_space=pltpu.SMEM)]
        + [pl.BlockSpec(memory_space=pltpu.VMEM)] * (len(pieces) + 1),
        out_specs=pl.BlockSpec(memory_space=pltpu.VMEM),
        out_shape=jax.ShapeDtypeStruct((width_x, rank), F32),
        scratch_shapes=[pltpu.VMEM((width_x, width_x), F32)],
        compiler_params=pltpu.CompilerParams(vmem_limit_bytes=24 * MIB),
        cost_estimate=pl.CostEstimate(
            flops=4 * 10**10, bytes_accessed=8 * start.size, transcendentals=0
        ),
        name="subspace",
    )(places, *pieces, start)


def stack_body(places_ref, *refs):
    *piece_refs, out_ref = refs
    for i, piece_ref in enumerate(piece_refs):
        out_ref[places_ref[i]] = piece_ref[...]


def stack(pieces, places):
    return pl.pallas_call(
        stack_body,
        in_specs=[pl.BlockSpec(memory_space=pltpu.SMEM)]
        + [pl.BlockSpec(memory_space=pltpu.VMEM)] * len(pieces),
        out_specs=pl.BlockSpec(memory_space=pltpu.VMEM),
        out_shape=jax.ShapeDtypeStruct((len(pieces),) + pieces[0].shape, F32),
        compiler_params=pltpu.CompilerParams(vmem_limit_bytes=16 * MIB),
        name="stack_rows",
    )(places, *pieces)


def pack_body(first_ref, field_ref, out_ref):
    for z in range(field_ref.shape[1]):
        out_ref[z] = field_ref[:, z, :]


def pack(field, first, depth):
    x_block, _, y_block = field.shape
    return pl.pallas_call(
        pack_body,
        grid_spec=pltpu.PrefetchScalarGridSpec(
            num_scalar_prefetch=1,
            grid=(depth // TALL,),
            in_specs=[pl.BlockSpec((x_block, TALL, y_block), lambda i, at: (0, at[0] + i, 0))],
            out_specs=pl.BlockSpec((TALL, x_block, y_block), lambda i, at: (i, 0, 0)),
        ),
        out_shape=jax.ShapeDtypeStruct((depth, x_block, y_block), F32),
        compiler_params=pltpu.CompilerParams(vmem_limit_bytes=48 * MIB),
        cost_estimate=pl.CostEstimate(
            flops=0, bytes_accessed=8 * depth * x_block * y_block, transcendentals=0
        ),
        name="pack_z",
    )(first.astype(jnp.int32).reshape(1), field)


def tie(value, others):
    return lax.optimization_barrier((value, *others))[0] if others else value


class Line:
    def __init__(self):
        self.ends = []

    def done(self, ahead):
        last = len(self.ends) - WINDOW + 1 - ahead
        return self.ends[max(0, last - 1) : max(0, last)]

    def send(self, cut, source, axis, perm):
        value = cut(tie(source, self.done(AHEAD)))
        got = lax.ppermute(tie(value, self.done(0)), axis, perm)
        self.ends.append(got)
        return got


def chunk_depths(groups):
    if groups < 4:
        return [groups]
    last = max(1, groups // 8)
    left = groups - 2 * last
    first = [(left + k) // 3 for k in (2, 1, 0)]
    return [depth for depth in first if depth] + [last, last]


def on_device(field, start):
    n = lax.axis_size("gx")
    m = lax.axis_size("yz")
    g = lax.axis_index("gx")
    q = lax.axis_index("yz")
    x_block, depth, y_block = field.shape
    width_x, width_y = x_block * n, y_block * m
    rank = start.shape[1]
    slab = depth // n
    line = LINE if n % LINE == 0 else 1
    rest = n // line
    order = Line()

    def moved(index, a, b, sign=1):
        return (index // rest + sign * a) % line * rest + (index % rest + sign * b) % rest

    def gx_perm(a, b):
        return [(i, moved(i, a, b)) for i in range(n)]

    def yz_perm(d):
        return [(i, (i + d) % m) for i in range(m)]

    far = sorted(range(1, line), key=lambda a: abs(2 * a - line))
    shifts = [(a, (b + k) % rest) for b in range(rest) for k, a in enumerate(far)]
    shifts[4:4] = [(0, b) for b in range(1, rest)]
    turns = sorted(range(1, m), key=lambda d: abs(2 * d - m))


    def to_gx(first, zc, a, b, whole):
        place = (moved(g, a, b) * slab + first) // TALL
        got = order.send(lambda at: pack(field, at, zc), place, "gx", gx_perm(a, b))
        return lax.dynamic_update_slice_in_dim(whole, got[:, None], moved(g, a, b, -1), axis=1)

    def to_yz(cells, first, d, whole, after=()):
        zs = whole.shape[0] // m

        def cut(source):
            return lax.dynamic_slice_in_dim(source, (q + d) % m * zs, zs, axis=0)

        got = order.send(cut, tie(whole, after), "yz", yz_perm(d))
        return lax.dynamic_update_slice(cells, got[:, None], (first // m, (q - d) % m, 0, 0))

    def put_own(cells, first, whole):
        zs = whole.shape[0] // m
        own = lax.dynamic_slice_in_dim(whole, q * zs, zs, axis=0)
        return lax.dynamic_update_slice(cells, own[:, None], (first // m, q, 0, 0))

    gram = jnp.zeros((width_x, width_x), F32)
    first, waiting = 0, []
    group = math.lcm(m, TALL)
    depths = chunk_depths(slab // group)
    start_last = (sum(depths) - depths[-1]) * group
    cells = jnp.zeros((start_last // m, m, width_x, y_block), F32)
    for groups in depths:
        zc = groups * group
        whole = jnp.zeros((zc, n, x_block, y_block), F32)
        for k, (a, b) in enumerate(shifts):
            whole = to_gx(first, zc, a, b, whole)
            if k % 3 == 1 or k == len(shifts) - 1:
                if waiting and (k >= WINDOW - 1 or len(waiting) > len(turns)):
                    cells = to_yz(cells, *waiting.pop(0))
        own = pack(field, (g * slab + first) // TALL, zc)[:, None]
        whole = lax.dynamic_update_slice_in_dim(whole, own, g, axis=1)
        before = whole.reshape(zc, width_x, y_block)
        gram = gram_of(before, gram)
        if first < start_last:
            cells = put_own(cells, first, before)
            waiting += [(first, d, before) for d in turns]
            first += zc

    rows = width_x // m
    slabs = gram.reshape(m, rows, width_x)

    def pick(array, index):
        return lax.dynamic_index_in_dim(array, index, axis=0, keepdims=False)

    summed = pick(slabs, q)
    for d in turns:
        summed = summed + lax.ppermute(pick(slabs, (q + d) % m), "yz", yz_perm(d))
    for entry in waiting:
        cells = to_yz(cells, *entry)
    strips = summed.reshape(n, rows // n, width_x)
    summed = pick(strips, g)
    for a, b in shifts:
        summed = summed + lax.ppermute(pick(strips, moved(g, a, b)), "gx", gx_perm(a, b))
    pieces = [summed] + [lax.ppermute(summed, "gx", gx_perm(a, b)) for a, b in shifts]
    places = jnp.stack([g] + [moved(g, a, b, -1) for a, b in shifts]).astype(jnp.int32)
    summed = stack(pieces, places).reshape(rows, width_x)
    pieces = [summed] + [lax.ppermute(summed, "yz", yz_perm(d)) for d in turns]
    places = jnp.stack([q] + [(q - d) % m for d in turns]).astype(jnp.int32)
    ready = pieces[1:]
    basis = iterate(pieces, places, start, float(width_y * depth))

    sums = core_gram(cells, basis) if start_last else ()
    cells = jnp.zeros((before.shape[0] // m, m, width_x, y_block), F32)
    cells = put_own(cells, 0, before)
    for d in turns:
        cells = to_yz(cells, 0, d, before, ready)
    partial_y = core_gram(cells, basis, sums, float(rank * depth))
    cores = 2 if m % 2 == 0 else 1
    chips = m // cores
    core, chip = q % cores, q // cores
    blocks = partial_y.reshape(chips, cores, y_block, width_y)

    def of_core(index):
        return lax.dynamic_index_in_dim(blocks, index, axis=1, keepdims=False)

    blocks_here = of_core(core)
    for d in range(1, cores):
        perm = [(i, i // cores * cores + (i + d) % cores) for i in range(m)]
        blocks_here = blocks_here + lax.ppermute(of_core((core + d) % cores), "yz", perm)
    rows_y = pick(blocks_here, chip)
    for d in range(1, chips):
        perm = [(i, (i + d * cores) % m) for i in range(m)]
        rows_y = rows_y + lax.ppermute(pick(blocks_here, (chip + d) % chips), "yz", perm)
    width = width_y // n

    def block(index):
        return lax.dynamic_slice_in_dim(rows_y, index * width, width, axis=1)

    gram_y = block(g)
    for a, b in shifts:
        gram_y = gram_y + lax.ppermute(block(moved(g, a, b)), "gx", gx_perm(a, b))
    return (basis, gram_y)


def solution(mesh):
    placed = (P("gx", None, "yz"), P())
    return jax.shard_map(
        on_device, mesh=mesh, in_specs=placed, out_specs=(P(), P("yz", "gx")), check_vma=False
    )
```

```python
import functools
import math

import jax
import jax.numpy as jnp
from jax import lax
from jax.experimental import pallas as pl
from jax.experimental.pallas import tpu as pltpu
from jax.sharding import PartitionSpec as P

ITERS = 4
WINDOW = 5
AHEAD = 2
TALL = 8
LINE = 4
MIB = 1024 * 1024
F32 = jnp.float32
BF16 = jnp.bfloat16


def halves(value):
    high = value.astype(BF16)
    low = (value - high.astype(F32)).astype(BF16)
    return high, low


def dot_nt(left, right):
    return lax.dot_general(left, right, (((1,), (1,)), ((), ())), preferred_element_type=F32)


def dot_tn(left, right):
    return lax.dot_general(left, right, (((0,), (0,)), ((), ())), preferred_element_type=F32)


def gram_body(steps, slab_ref, before_ref, out_ref, main, cross):
    step = pl.program_id(0)

    @pl.when(step == 0)
    def _():
        main[...] = jnp.zeros_like(main)
        cross[...] = jnp.zeros_like(cross)

    depth = slab_ref.shape[0]
    parts = [halves(slab_ref[z]) for z in range(depth)]
    high = jnp.concatenate([part[0] for part in parts], axis=1)
    low = jnp.concatenate([part[1] for part in parts], axis=1)
    main[...] += dot_nt(high, high)
    cross[...] += dot_nt(high, low)

    @pl.when(step == steps - 1)
    def _():
        mixed = cross[...]
        out_ref[...] = before_ref[...] + main[...] + mixed + mixed.T


def gram_of(slab, before):
    depth, width_x, width_y = slab.shape
    block = 4 if depth % 4 == 0 else 1
    steps = depth // block
    square = pl.BlockSpec((width_x, width_x), lambda i: (0, 0))
    return pl.pallas_call(
        functools.partial(gram_body, steps),
        grid=(steps,),
        in_specs=[pl.BlockSpec((block, width_x, width_y), lambda i: (i, 0, 0)), square],
        out_specs=square,
        out_shape=jax.ShapeDtypeStruct((width_x, width_x), F32),
        scratch_shapes=[pltpu.VMEM((width_x, width_x), F32)] * 2,
        compiler_params=pltpu.CompilerParams(vmem_limit_bytes=32 * MIB),
        cost_estimate=pl.CostEstimate(
            flops=4 * width_x * width_x * depth * width_y,
            bytes_accessed=slab.size * 4,
            transcendentals=0,
        ),
        name="gram_x",
    )(slab, before)


def core_body(steps, total, field_ref, basis_ref, out_ref, stacked_ref, high_ref, low_ref, main, cross):
    step = pl.program_id(0)
    rank = basis_ref.shape[1]

    @pl.when(step == 0)
    def _():
        main[...] = jnp.zeros_like(main)
        cross[...] = jnp.zeros_like(cross)
        basis_high, basis_low = halves(basis_ref[...].T)
        stacked_ref[:rank] = basis_high
        stacked_ref[rank:] = basis_low

    depth, blocks, _, width = field_ref.shape
    stacked = stacked_ref[...]
    for z in range(depth):
        for b in range(blocks):
            high, low = halves(field_ref[z, b])
            both = jnp.dot(stacked, high, preferred_element_type=F32)
            core = both[:rank] + both[rank:]
            core += jnp.dot(stacked[:rank], low, preferred_element_type=F32)
            core_high, core_low = halves(core)
            high_ref[pl.ds(z * rank, rank), pl.ds(b * width, width)] = core_high
            low_ref[pl.ds(z * rank, rank), pl.ds(b * width, width)] = core_low
    high = high_ref[...]
    main[...] += dot_tn(high, high)
    cross[...] += dot_tn(high, low_ref[...])

    @pl.when(step == steps - 1)
    def _():
        mixed = cross[...]
        out_ref[...] = (main[...] + mixed + mixed.T) / total


def core_gram(cells, basis, total):
    depth, blocks, width_x, width = cells.shape
    rank = basis.shape[1]
    width_y = blocks * width
    block = 2 if depth % 2 == 0 else 1
    steps = depth // block
    return pl.pallas_call(
        functools.partial(core_body, steps, total),
        grid=(steps,),
        in_specs=[
            pl.BlockSpec((block, blocks, width_x, width), lambda i: (i, 0, 0, 0)),
            pl.BlockSpec((width_x, rank), lambda i: (0, 0)),
        ],
        out_specs=pl.BlockSpec((width_y, width_y), lambda i: (0, 0)),
        out_shape=jax.ShapeDtypeStruct((width_y, width_y), F32),
        scratch_shapes=[
            pltpu.VMEM((2 * rank, width_x), BF16),
            pltpu.VMEM((block * rank, width_y), BF16),
            pltpu.VMEM((block * rank, width_y), BF16),
            pltpu.VMEM((width_y, width_y), F32),
            pltpu.VMEM((width_y, width_y), F32),
        ],
        compiler_params=pltpu.CompilerParams(vmem_limit_bytes=48 * MIB),
        cost_estimate=pl.CostEstimate(
            flops=6 * rank * cells.size + 4 * rank * depth * width_y * width_y,
            bytes_accessed=cells.size * 4,
            transcendentals=0,
        ),
        name="core_gram_y",
    )(cells, basis)


def full_dot(left, right, contract):
    return lax.dot_general(
        left,
        right,
        ((contract[:1], contract[1:]), ((), ())),
        precision=lax.Precision.HIGHEST,
        preferred_element_type=F32,
    )


def inverse_factor(cross):
    size = cross.shape[0]
    tall = 8
    wide = 4
    groups = size // tall
    shape = (tall, size)
    sublane = lax.broadcasted_iota(jnp.int32, shape, 0)
    lane = lax.broadcasted_iota(jnp.int32, shape, 1)
    left = [cross[t * tall : (t + 1) * tall] for t in range(groups)]
    right = [(lane == sublane + t * tall).astype(F32) for t in range(groups)]
    pivots = [jnp.ones(shape, F32) for _ in range(groups)]

    def row(value, s):
        return jnp.broadcast_to(value[s : s + 1, :], shape)

    for first in range(0, size, wide):
        top, s0 = first // tall, first % tall
        below = range(top, groups)
        columns = [
            {t: jnp.broadcast_to(left[t][:, first + k : first + k + 1], shape) for t in below}
            for k in range(wide)
        ]
        rows = [row(left[top], s0 + k) for k in range(wide)]
        eyes = [row(right[top], s0 + k) for k in range(wide)]
        scaled = []
        for i in range(wide):
            pivot = row(columns[i][top], s0 + i)
            inverse = 1.0 / pivot
            scaled.append((rows[i] * inverse, eyes[i] * inverse))
            for k in range(i + 1, wide):
                ratio = row(columns[i][top], s0 + k) * inverse
                for t in below:
                    columns[k][t] = columns[k][t] - ratio * columns[i][t]
                rows[k] = rows[k] - ratio * rows[i]
                eyes[k] = eyes[k] - ratio * eyes[i]
            here = sublane == s0 + i
            pivots[top] = jnp.where(here, pivot, pivots[top])
        rest = sublane >= s0 + wide
        for t in below:
            new_left, new_right = left[t], right[t]
            for i in range(wide):
                new_left = new_left - columns[i][t] * scaled[i][0]
                new_right = new_right - columns[i][t] * scaled[i][1]
            if t == top:
                new_left = jnp.where(rest, new_left, left[t])
                new_right = jnp.where(rest, new_right, right[t])
                for i in range(wide):
                    new_right = jnp.where(sublane == s0 + i, eyes[i], new_right)
            left[t], right[t] = new_left, new_right
    for t in range(groups):
        root = lax.rsqrt(pivots[t])
        root = root * (1.5 - 0.5 * pivots[t] * root * root)
        right[t] = right[t] * root
    return jnp.concatenate(right, axis=0)


def iterate_body(total, places_ref, *refs):
    *piece_refs, start_ref, out_ref, gram = refs
    height = piece_refs[0].shape[0]
    for i, piece_ref in enumerate(piece_refs):
        place = pl.multiple_of(places_ref[i] * height, height)
        gram[pl.ds(place, height)] = piece_ref[...] / total
    out_ref[...] = start_ref[...]

    def step(_, carry):
        product = full_dot(gram[...], out_ref[...], (1, 0))
        inverse = inverse_factor(full_dot(product, product, (0, 0)))
        out_ref[...] = full_dot(product, inverse, (1, 1))
        return carry

    lax.fori_loop(0, ITERS, step, 0)


def iterate(pieces, places, start, total):
    width_x, rank = start.shape
    return pl.pallas_call(
        functools.partial(iterate_body, total),
        in_specs=[pl.BlockSpec(memory_space=pltpu.SMEM)]
        + [pl.BlockSpec(memory_space=pltpu.VMEM)] * (len(pieces) + 1),
        out_specs=pl.BlockSpec(memory_space=pltpu.VMEM),
        out_shape=jax.ShapeDtypeStruct((width_x, rank), F32),
        scratch_shapes=[pltpu.VMEM((width_x, width_x), F32)],
        compiler_params=pltpu.CompilerParams(vmem_limit_bytes=24 * MIB),
        cost_estimate=pl.CostEstimate(
            flops=4 * 10**10, bytes_accessed=8 * start.size, transcendentals=0
        ),
        name="subspace",
    )(places, *pieces, start)


def stack_body(places_ref, *refs):
    *piece_refs, out_ref = refs
    for i, piece_ref in enumerate(piece_refs):
        out_ref[places_ref[i]] = piece_ref[...]


def stack(pieces, places):
    return pl.pallas_call(
        stack_body,
        in_specs=[pl.BlockSpec(memory_space=pltpu.SMEM)]
        + [pl.BlockSpec(memory_space=pltpu.VMEM)] * len(pieces),
        out_specs=pl.BlockSpec(memory_space=pltpu.VMEM),
        out_shape=jax.ShapeDtypeStruct((len(pieces),) + pieces[0].shape, F32),
        compiler_params=pltpu.CompilerParams(vmem_limit_bytes=16 * MIB),
        name="stack_rows",
    )(places, *pieces)


def pack_body(first_ref, field_ref, out_ref):
    for z in range(field_ref.shape[1]):
        out_ref[z] = field_ref[:, z, :]


def pack(field, first, depth):
    x_block, _, y_block = field.shape
    return pl.pallas_call(
        pack_body,
        grid_spec=pltpu.PrefetchScalarGridSpec(
            num_scalar_prefetch=1,
            grid=(depth // TALL,),
            in_specs=[pl.BlockSpec((x_block, TALL, y_block), lambda i, at: (0, at[0] + i, 0))],
            out_specs=pl.BlockSpec((TALL, x_block, y_block), lambda i, at: (i, 0, 0)),
        ),
        out_shape=jax.ShapeDtypeStruct((depth, x_block, y_block), F32),
        compiler_params=pltpu.CompilerParams(vmem_limit_bytes=48 * MIB),
        cost_estimate=pl.CostEstimate(
            flops=0, bytes_accessed=8 * depth * x_block * y_block, transcendentals=0
        ),
        name="pack_z",
    )(first.astype(jnp.int32).reshape(1), field)


def tie(value, others):
    return lax.optimization_barrier((value, *others))[0] if others else value


class Line:
    def __init__(self):
        self.ends = []

    def done(self, ahead):
        last = len(self.ends) - WINDOW + 1 - ahead
        return self.ends[max(0, last - 1) : max(0, last)]

    def send(self, cut, source, axis, perm):
        value = cut(tie(source, self.done(AHEAD)))
        got = lax.ppermute(tie(value, self.done(0)), axis, perm)
        self.ends.append(got)
        return got


def chunk_depths(groups):
    if groups < 4:
        return [groups]
    last = max(1, groups // 8)
    left = groups - 2 * last
    first = [(left + k) // 3 for k in (2, 1, 0)]
    return [depth for depth in first if depth] + [last, last]


def on_device(field, start):
    n = lax.axis_size("gx")
    m = lax.axis_size("yz")
    g = lax.axis_index("gx")
    q = lax.axis_index("yz")
    x_block, depth, y_block = field.shape
    width_x, width_y = x_block * n, y_block * m
    rank = start.shape[1]
    slab = depth // n
    line = LINE if n % LINE == 0 else 1
    rest = n // line
    order = Line()

    def moved(index, a, b, sign=1):
        return (index // rest + sign * a) % line * rest + (index % rest + sign * b) % rest

    def gx_perm(a, b):
        return [(i, moved(i, a, b)) for i in range(n)]

    def yz_perm(d):
        return [(i, (i + d) % m) for i in range(m)]

    far = sorted(range(1, line), key=lambda a: abs(2 * a - line))
    shifts = [(a, (b + k) % rest) for b in range(rest) for k, a in enumerate(far)]
    shifts[4:4] = [(0, b) for b in range(1, rest)]
    turns = sorted(range(1, m), key=lambda d: abs(2 * d - m))

    cells = jnp.zeros((slab // m, m, width_x, y_block), F32)

    def to_gx(first, zc, a, b, whole):
        place = (moved(g, a, b) * slab + first) // TALL
        got = order.send(lambda at: pack(field, at, zc), place, "gx", gx_perm(a, b))
        return lax.dynamic_update_slice_in_dim(whole, got[:, None], moved(g, a, b, -1), axis=1)

    def to_yz(cells, first, d, whole, after=()):
        zs = whole.shape[0] // m

        def cut(source):
            return lax.dynamic_slice_in_dim(source, (q + d) % m * zs, zs, axis=0)

        got = order.send(cut, tie(whole, after), "yz", yz_perm(d))
        crossed.append(got)
        return lax.dynamic_update_slice(cells, got[:, None], (first // m, (q - d) % m, 0, 0))

    gram = jnp.zeros((width_x, width_x), F32)
    first, waiting = 0, []
    crossed = []
    group = math.lcm(m, TALL)
    for groups in chunk_depths(slab // group):
        zc = groups * group
        units = zc // m
        whole = jnp.zeros((zc, n, x_block, y_block), F32)
        for k, (a, b) in enumerate(shifts):
            whole = to_gx(first, zc, a, b, whole)
            if k % 3 == 1 or k == len(shifts) - 1:
                if waiting and (k >= WINDOW - 1 or len(waiting) > len(turns)):
                    cells = to_yz(cells, *waiting.pop(0))
        own = pack(field, (g * slab + first) // TALL, zc)[:, None]
        whole = lax.dynamic_update_slice_in_dim(whole, own, g, axis=1)
        before = whole.reshape(zc, width_x, y_block)
        gram = gram_of(before, gram)
        own = lax.dynamic_slice_in_dim(before, q * units, units, axis=0)
        cells = lax.dynamic_update_slice(cells, own[:, None], (first // m, q, 0, 0))
        waiting += [(first, d, before) for d in turns]
        first += zc

    rows = width_x // m
    slabs = gram.reshape(m, rows, width_x)

    def pick(array, index):
        return lax.dynamic_index_in_dim(array, index, axis=0, keepdims=False)

    summed = pick(slabs, q)
    for d in turns:
        summed = summed + lax.ppermute(pick(slabs, (q + d) % m), "yz", yz_perm(d))
    while len(waiting) > len(turns):
        cells = to_yz(cells, *waiting.pop(0))
    earlier = crossed[-len(turns) :]
    strips = summed.reshape(n, rows // n, width_x)
    summed = pick(strips, g)
    for a, b in shifts:
        summed = summed + lax.ppermute(pick(strips, moved(g, a, b)), "gx", gx_perm(a, b))
    summed = tie(summed, earlier)
    pieces = [summed] + [lax.ppermute(summed, "gx", gx_perm(a, b)) for a, b in shifts]
    places = jnp.stack([g] + [moved(g, a, b, -1) for a, b in shifts]).astype(jnp.int32)
    summed = stack(pieces, places).reshape(rows, width_x)
    pieces = [summed] + [lax.ppermute(summed, "yz", yz_perm(d)) for d in turns]
    places = jnp.stack([q] + [(q - d) % m for d in turns]).astype(jnp.int32)
    for entry in waiting:
        cells = to_yz(cells, *entry, pieces[1:])
    basis = iterate(pieces, places, start, float(width_y * depth))

    partial_y = core_gram(cells, basis, float(rank * depth))
    cores = 2 if m % 2 == 0 else 1
    chips = m // cores
    core, chip = q % cores, q // cores
    blocks = partial_y.reshape(chips, cores, y_block, width_y)

    def of_core(index):
        return lax.dynamic_index_in_dim(blocks, index, axis=1, keepdims=False)

    blocks_here = of_core(core)
    for d in range(1, cores):
        perm = [(i, i // cores * cores + (i + d) % cores) for i in range(m)]
        blocks_here = blocks_here + lax.ppermute(of_core((core + d) % cores), "yz", perm)
    rows_y = pick(blocks_here, chip)
    for d in range(1, chips):
        perm = [(i, (i + d * cores) % m) for i in range(m)]
        rows_y = rows_y + lax.ppermute(pick(blocks_here, (chip + d) % chips), "yz", perm)
    width = width_y // n

    def block(index):
        return lax.dynamic_slice_in_dim(rows_y, index * width, width, axis=1)

    gram_y = block(g)
    for a, b in shifts:
        gram_y = gram_y + lax.ppermute(block(moved(g, a, b)), "gx", gx_perm(a, b))
    return (basis, gram_y)


def solution(mesh):
    placed = (P("gx", None, "yz"), P())
    return jax.shard_map(
        on_device, mesh=mesh, in_specs=placed, out_specs=(P(), P("yz", "gx")), check_vma=False
    )
```

```python
import functools
import math

import jax
import jax.numpy as jnp
from jax import lax
from jax.experimental import pallas as pl
from jax.experimental.pallas import tpu as pltpu
from jax.sharding import PartitionSpec as P

ITERS = 4
WINDOW = 5
AHEAD = 2
TALL = 8
LINE = 4
MIB = 1024 * 1024
F32 = jnp.float32
BF16 = jnp.bfloat16


def halves(value):
    high = value.astype(BF16)
    low = (value - high.astype(F32)).astype(BF16)
    return high, low


def dot_nt(left, right):
    return lax.dot_general(left, right, (((1,), (1,)), ((), ())), preferred_element_type=F32)


def dot_tn(left, right):
    return lax.dot_general(left, right, (((0,), (0,)), ((), ())), preferred_element_type=F32)


def gram_body(steps, slab_ref, before_ref, out_ref, main, cross):
    step = pl.program_id(0)

    @pl.when(step == 0)
    def _():
        main[...] = jnp.zeros_like(main)
        cross[...] = jnp.zeros_like(cross)

    depth = slab_ref.shape[0]
    parts = [halves(slab_ref[z]) for z in range(depth)]
    high = jnp.concatenate([part[0] for part in parts], axis=1)
    low = jnp.concatenate([part[1] for part in parts], axis=1)
    main[...] += dot_nt(high, high)
    cross[...] += dot_nt(high, low)

    @pl.when(step == steps - 1)
    def _():
        mixed = cross[...]
        out_ref[...] = before_ref[...] + main[...] + mixed + mixed.T


def gram_of(slab, before):
    depth, width_x, width_y = slab.shape
    block = 4 if depth % 4 == 0 else 1
    steps = depth // block
    square = pl.BlockSpec((width_x, width_x), lambda i: (0, 0))
    return pl.pallas_call(
        functools.partial(gram_body, steps),
        grid=(steps,),
        in_specs=[pl.BlockSpec((block, width_x, width_y), lambda i: (i, 0, 0)), square],
        out_specs=square,
        out_shape=jax.ShapeDtypeStruct((width_x, width_x), F32),
        scratch_shapes=[pltpu.VMEM((width_x, width_x), F32)] * 2,
        compiler_params=pltpu.CompilerParams(vmem_limit_bytes=32 * MIB),
        cost_estimate=pl.CostEstimate(
            flops=4 * width_x * width_x * depth * width_y,
            bytes_accessed=slab.size * 4,
            transcendentals=0,
        ),
        name="gram_x",
    )(slab, before)


def core_body(steps, total, field_ref, basis_ref, out_ref, stacked_ref, high_ref, low_ref, main, cross):
    step = pl.program_id(0)
    rank = basis_ref.shape[1]

    @pl.when(step == 0)
    def _():
        main[...] = jnp.zeros_like(main)
        cross[...] = jnp.zeros_like(cross)
        basis_high, basis_low = halves(basis_ref[...].T)
        stacked_ref[:rank] = basis_high
        stacked_ref[rank:] = basis_low

    depth, blocks, _, width = field_ref.shape
    stacked = stacked_ref[...]
    for z in range(depth):
        for b in range(blocks):
            high, low = halves(field_ref[z, b])
            both = jnp.dot(stacked, high, preferred_element_type=F32)
            core = both[:rank] + both[rank:]
            core += jnp.dot(stacked[:rank], low, preferred_element_type=F32)
            core_high, core_low = halves(core)
            high_ref[pl.ds(z * rank, rank), pl.ds(b * width, width)] = core_high
            low_ref[pl.ds(z * rank, rank), pl.ds(b * width, width)] = core_low
    high = high_ref[...]
    main[...] += dot_tn(high, high)
    cross[...] += dot_tn(high, low_ref[...])

    @pl.when(step == steps - 1)
    def _():
        mixed = cross[...]
        out_ref[...] = (main[...] + mixed + mixed.T) / total


def core_gram(cells, basis, total):
    depth, blocks, width_x, width = cells.shape
    rank = basis.shape[1]
    width_y = blocks * width
    block = 4 if depth % 4 == 0 else 1
    steps = depth // block
    return pl.pallas_call(
        functools.partial(core_body, steps, total),
        grid=(steps,),
        in_specs=[
            pl.BlockSpec((block, blocks, width_x, width), lambda i: (i, 0, 0, 0)),
            pl.BlockSpec((width_x, rank), lambda i: (0, 0)),
        ],
        out_specs=pl.BlockSpec((width_y, width_y), lambda i: (0, 0)),
        out_shape=jax.ShapeDtypeStruct((width_y, width_y), F32),
        scratch_shapes=[
            pltpu.VMEM((2 * rank, width_x), BF16),
            pltpu.VMEM((block * rank, width_y), BF16),
            pltpu.VMEM((block * rank, width_y), BF16),
            pltpu.VMEM((width_y, width_y), F32),
            pltpu.VMEM((width_y, width_y), F32),
        ],
        compiler_params=pltpu.CompilerParams(vmem_limit_bytes=56 * MIB),
        cost_estimate=pl.CostEstimate(
            flops=6 * rank * cells.size + 4 * rank * depth * width_y * width_y,
            bytes_accessed=cells.size * 4,
            transcendentals=0,
        ),
        name="core_gram_y",
    )(cells, basis)


def full_dot(left, right, contract):
    return lax.dot_general(
        left,
        right,
        ((contract[:1], contract[1:]), ((), ())),
        precision=lax.Precision.HIGHEST,
        preferred_element_type=F32,
    )


def inverse_factor(cross):
    size = cross.shape[0]
    tall = 8
    wide = 4
    groups = size // tall
    shape = (tall, size)
    sublane = lax.broadcasted_iota(jnp.int32, shape, 0)
    lane = lax.broadcasted_iota(jnp.int32, shape, 1)
    left = [cross[t * tall : (t + 1) * tall] for t in range(groups)]
    right = [(lane == sublane + t * tall).astype(F32) for t in range(groups)]
    pivots = [jnp.ones(shape, F32) for _ in range(groups)]

    def row(value, s):
        return jnp.broadcast_to(value[s : s + 1, :], shape)

    for first in range(0, size, wide):
        top, s0 = first // tall, first % tall
        below = range(top, groups)
        columns = [
            {t: jnp.broadcast_to(left[t][:, first + k : first + k + 1], shape) for t in below}
            for k in range(wide)
        ]
        rows = [row(left[top], s0 + k) for k in range(wide)]
        eyes = [row(right[top], s0 + k) for k in range(wide)]
        scaled = []
        for i in range(wide):
            pivot = row(columns[i][top], s0 + i)
            inverse = 1.0 / pivot
            scaled.append((rows[i] * inverse, eyes[i] * inverse))
            for k in range(i + 1, wide):
                ratio = row(columns[i][top], s0 + k) * inverse
                for t in below:
                    columns[k][t] = columns[k][t] - ratio * columns[i][t]
                rows[k] = rows[k] - ratio * rows[i]
                eyes[k] = eyes[k] - ratio * eyes[i]
            here = sublane == s0 + i
            pivots[top] = jnp.where(here, pivot, pivots[top])
        rest = sublane >= s0 + wide
        for t in below:
            new_left, new_right = left[t], right[t]
            for i in range(wide):
                new_left = new_left - columns[i][t] * scaled[i][0]
                new_right = new_right - columns[i][t] * scaled[i][1]
            if t == top:
                new_left = jnp.where(rest, new_left, left[t])
                new_right = jnp.where(rest, new_right, right[t])
                for i in range(wide):
                    new_right = jnp.where(sublane == s0 + i, eyes[i], new_right)
            left[t], right[t] = new_left, new_right
    for t in range(groups):
        root = lax.rsqrt(pivots[t])
        root = root * (1.5 - 0.5 * pivots[t] * root * root)
        right[t] = right[t] * root
    return jnp.concatenate(right, axis=0)


def iterate_body(total, places_ref, *refs):
    *piece_refs, start_ref, out_ref, gram = refs
    height = piece_refs[0].shape[0]
    for i, piece_ref in enumerate(piece_refs):
        place = pl.multiple_of(places_ref[i] * height, height)
        gram[pl.ds(place, height)] = piece_ref[...] / total
    out_ref[...] = start_ref[...]

    def step(_, carry):
        product = full_dot(gram[...], out_ref[...], (1, 0))
        inverse = inverse_factor(full_dot(product, product, (0, 0)))
        out_ref[...] = full_dot(product, inverse, (1, 1))
        return carry

    lax.fori_loop(0, ITERS, step, 0)


def iterate(pieces, places, start, total):
    width_x, rank = start.shape
    return pl.pallas_call(
        functools.partial(iterate_body, total),
        in_specs=[pl.BlockSpec(memory_space=pltpu.SMEM)]
        + [pl.BlockSpec(memory_space=pltpu.VMEM)] * (len(pieces) + 1),
        out_specs=pl.BlockSpec(memory_space=pltpu.VMEM),
        out_shape=jax.ShapeDtypeStruct((width_x, rank), F32),
        scratch_shapes=[pltpu.VMEM((width_x, width_x), F32)],
        compiler_params=pltpu.CompilerParams(vmem_limit_bytes=24 * MIB),
        cost_estimate=pl.CostEstimate(
            flops=4 * 10**10, bytes_accessed=8 * start.size, transcendentals=0
        ),
        name="subspace",
    )(places, *pieces, start)


def stack_body(places_ref, *refs):
    *piece_refs, out_ref = refs
    for i, piece_ref in enumerate(piece_refs):
        out_ref[places_ref[i]] = piece_ref[...]


def stack(pieces, places):
    return pl.pallas_call(
        stack_body,
        in_specs=[pl.BlockSpec(memory_space=pltpu.SMEM)]
        + [pl.BlockSpec(memory_space=pltpu.VMEM)] * len(pieces),
        out_specs=pl.BlockSpec(memory_space=pltpu.VMEM),
        out_shape=jax.ShapeDtypeStruct((len(pieces),) + pieces[0].shape, F32),
        compiler_params=pltpu.CompilerParams(vmem_limit_bytes=16 * MIB),
        name="stack_rows",
    )(places, *pieces)


def pack_body(first_ref, field_ref, out_ref):
    for z in range(field_ref.shape[1]):
        out_ref[z] = field_ref[:, z, :]


def pack(field, first, depth):
    x_block, _, y_block = field.shape
    return pl.pallas_call(
        pack_body,
        grid_spec=pltpu.PrefetchScalarGridSpec(
            num_scalar_prefetch=1,
            grid=(depth // TALL,),
            in_specs=[pl.BlockSpec((x_block, TALL, y_block), lambda i, at: (0, at[0] + i, 0))],
            out_specs=pl.BlockSpec((TALL, x_block, y_block), lambda i, at: (i, 0, 0)),
        ),
        out_shape=jax.ShapeDtypeStruct((depth, x_block, y_block), F32),
        compiler_params=pltpu.CompilerParams(vmem_limit_bytes=48 * MIB),
        cost_estimate=pl.CostEstimate(
            flops=0, bytes_accessed=8 * depth * x_block * y_block, transcendentals=0
        ),
        name="pack_z",
    )(first.astype(jnp.int32).reshape(1), field)


def tie(value, others):
    return lax.optimization_barrier((value, *others))[0] if others else value


class Line:
    def __init__(self):
        self.ends = []

    def done(self, ahead):
        last = len(self.ends) - WINDOW + 1 - ahead
        return self.ends[max(0, last - 1) : max(0, last)]

    def send(self, cut, source, axis, perm):
        value = cut(tie(source, self.done(AHEAD)))
        got = lax.ppermute(tie(value, self.done(0)), axis, perm)
        self.ends.append(got)
        return got


def chunk_depths(groups):
    if groups < 4:
        return [groups]
    last = max(1, groups // 8)
    left = groups - 2 * last
    first = [(left + k) // 3 for k in (2, 1, 0)]
    return [depth for depth in first if depth] + [last, last]


def on_device(field, start):
    n = lax.axis_size("gx")
    m = lax.axis_size("yz")
    g = lax.axis_index("gx")
    q = lax.axis_index("yz")
    x_block, depth, y_block = field.shape
    width_x, width_y = x_block * n, y_block * m
    rank = start.shape[1]
    slab = depth // n
    line = LINE if n % LINE == 0 else 1
    rest = n // line
    order = Line()

    def moved(index, a, b, sign=1):
        return (index // rest + sign * a) % line * rest + (index % rest + sign * b) % rest

    def gx_perm(a, b):
        return [(i, moved(i, a, b)) for i in range(n)]

    def yz_perm(d):
        return [(i, (i + d) % m) for i in range(m)]

    far = sorted(range(1, line), key=lambda a: abs(2 * a - line))
    shifts = [(a, (b + k) % rest) for b in range(rest) for k, a in enumerate(far)]
    shifts[4:4] = [(0, b) for b in range(1, rest)]
    turns = sorted(range(1, m), key=lambda d: abs(2 * d - m))

    cells = jnp.zeros((slab // m, m, width_x, y_block), F32)

    def to_gx(first, zc, a, b, whole):
        place = (moved(g, a, b) * slab + first) // TALL
        got = order.send(lambda at: pack(field, at, zc), place, "gx", gx_perm(a, b))
        return lax.dynamic_update_slice_in_dim(whole, got[:, None], moved(g, a, b, -1), axis=1)

    def to_yz(cells, first, d, whole, after=()):
        zs = whole.shape[0] // m

        def cut(source):
            return lax.dynamic_slice_in_dim(source, (q + d) % m * zs, zs, axis=0)

        got = order.send(cut, tie(whole, after), "yz", yz_perm(d))
        return lax.dynamic_update_slice(cells, got[:, None], (first // m, (q - d) % m, 0, 0))

    gram = jnp.zeros((width_x, width_x), F32)
    first, waiting = 0, []
    group = math.lcm(m, TALL)
    for groups in chunk_depths(slab // group):
        zc = groups * group
        units = zc // m
        whole = jnp.zeros((zc, n, x_block, y_block), F32)
        for k, (a, b) in enumerate(shifts):
            whole = to_gx(first, zc, a, b, whole)
            if k % 3 == 1 or k == len(shifts) - 1:
                if waiting and (k >= WINDOW - 1 or len(waiting) > len(turns)):
                    cells = to_yz(cells, *waiting.pop(0))
        own = pack(field, (g * slab + first) // TALL, zc)[:, None]
        whole = lax.dynamic_update_slice_in_dim(whole, own, g, axis=1)
        before = whole.reshape(zc, width_x, y_block)
        gram = gram_of(before, gram)
        own = lax.dynamic_slice_in_dim(before, q * units, units, axis=0)
        cells = lax.dynamic_update_slice(cells, own[:, None], (first // m, q, 0, 0))
        waiting += [(first, d, before) for d in turns]
        first += zc

    rows = width_x // m
    slabs = gram.reshape(m, rows, width_x)

    def pick(array, index):
        return lax.dynamic_index_in_dim(array, index, axis=0, keepdims=False)

    summed = pick(slabs, q)
    for d in turns:
        summed = summed + lax.ppermute(pick(slabs, (q + d) % m), "yz", yz_perm(d))
    while len(waiting) >= len(turns):
        cells = to_yz(cells, *waiting.pop(0), [summed])
    strips = summed.reshape(n, rows // n, width_x)
    summed = pick(strips, g)
    for a, b in shifts:
        summed = summed + lax.ppermute(pick(strips, moved(g, a, b)), "gx", gx_perm(a, b))
    pieces = [summed] + [lax.ppermute(summed, "gx", gx_perm(a, b)) for a, b in shifts]
    places = jnp.stack([g] + [moved(g, a, b, -1) for a, b in shifts]).astype(jnp.int32)
    summed = stack(pieces, places).reshape(rows, width_x)
    pieces = [summed] + [lax.ppermute(summed, "yz", yz_perm(d)) for d in turns]
    places = jnp.stack([q] + [(q - d) % m for d in turns]).astype(jnp.int32)
    for entry in waiting:
        cells = to_yz(cells, *entry, pieces[1:])
    basis = iterate(pieces, places, start, float(width_y * depth))

    partial_y = core_gram(cells, basis, float(rank * depth))
    cores = 2 if m % 2 == 0 else 1
    chips = m // cores
    core, chip = q % cores, q // cores
    blocks = partial_y.reshape(chips, cores, y_block, width_y)

    def of_core(index):
        return lax.dynamic_index_in_dim(blocks, index, axis=1, keepdims=False)

    blocks_here = of_core(core)
    for d in range(1, cores):
        perm = [(i, i // cores * cores + (i + d) % cores) for i in range(m)]
        blocks_here = blocks_here + lax.ppermute(of_core((core + d) % cores), "yz", perm)
    rows_y = pick(blocks_here, chip)
    for d in range(1, chips):
        perm = [(i, (i + d * cores) % m) for i in range(m)]
        rows_y = rows_y + lax.ppermute(pick(blocks_here, (chip + d) % chips), "yz", perm)
    width = width_y // n

    def block(index):
        return lax.dynamic_slice_in_dim(rows_y, index * width, width, axis=1)

    gram_y = block(g)
    for a, b in shifts:
        gram_y = gram_y + lax.ppermute(block(moved(g, a, b)), "gx", gx_perm(a, b))
    return (basis, gram_y)


def solution(mesh):
    placed = (P("gx", None, "yz"), P())
    return jax.shard_map(
        on_device, mesh=mesh, in_specs=placed, out_specs=(P(), P("yz", "gx")), check_vma=False
    )
```
